32 devices in a mesh: dp: 8 (over z, y), tensor: 4 (over x, core).
Axes of the slice: x: 2, y: 2, z: 4, core: 2. Of those that a mesh axis runs over, the one named last changes fastest.
Arguments:
- tokens: bfloat16 [4096, 1024], P(('dp', 'tensor')), may hold values from -6 to 6
- cotangent: bfloat16 [4096, 1024], P(('dp', 'tensor')), may hold values from -6 to 6
- seg_lengths: int32 [8, 4], P('dp'), may hold values from 0 to 512, as said below
- vectors: float32 [6, 1024], P(None, 'dp'), may hold values from -2 to 2
- w_qkv: bfloat16 [1024, 3, 1024], P('dp', None, 'tensor'), may hold values from -0.1875 to 0.1875
- qv_bias: float32 [2, 16, 64], P(None, 'tensor', 'dp'), may hold values from -3 to 3
- w_out: bfloat16 [1024, 1024], P('tensor', 'dp'), may hold values from -0.5 to 0.5
- w_up: bfloat16 [1024, 4096], P('dp', 'tensor'), may hold values from -0.1875 to 0.1875
- up_bias: float32 [16, 256], P('tensor', 'dp'), may hold values from -3 to 3
- w_down: bfloat16 [4096, 1024], P('tensor', 'dp'), may hold values from -0.125 to 0.125
Outputs:
- output: bfloat16 [4096, 1024], P(('dp', 'tensor'))
- grad_tokens: bfloat16 [4096, 1024], P(('dp', 'tensor'))
- grad_vectors: float32 [6, 1024], P(None, 'dp')
- grad_qkv: float32 [1024, 3, 1024], P('dp', None, 'tensor')
- grad_qv_bias: float32 [2, 16, 64], P(None, 'tensor', 'dp')
- grad_out: float32 [1024, 1024], P('tensor', 'dp')
- grad_up: float32 [1024, 4096], P('dp', 'tensor')
- grad_up_bias: float32 [16, 256], P('tensor', 'dp')
- grad_down: float32 [4096, 1024], P('tensor', 'dp')
The draws below stay inside these ranges and needn't reach their ends.
Inputs may be any that keep to these rules, and one draw needn't show every extreme that they name: `seg_lengths`: each row gives, in order, the lengths of the 4 documents that fill the 512 positions of one group; a row sums to 512; a zero is an empty document; the first document of every group is longer than 384.
All inputs are finite; a program needn't handle non-finite values.
Results may differ from the reference program's by a relative error of at most 0.03.
Values may be sent and summed in bfloat16 or wider, within the bound.
A program may use at most 64 MiB of HBM per device.

```python
import jax
import jax.numpy as jnp
from jax import lax

D = 1024
HEADS = 16
HD = 64
FF = 4096
TOK_DEV = 128
SEGS = 4
GROUP = 512
GROUPS = 8
TOKENS = 4096


def draw_seg_lengths(key, part):
    key = jax.random.fold_in(key, 11)
    key_long, key_pick, key_cuts = jax.random.split(key, 3)
    longest = jax.random.randint(key_long, (GROUPS,), GROUP - TOK_DEV + 1, GROUP + 1)
    chosen = jax.random.randint(key_pick, (), 0, GROUPS)
    longest = jnp.where(jnp.arange(GROUPS) == chosen, GROUP, longest)
    remainder = GROUP - longest
    cut_points = jax.random.randint(key_cuts, (GROUPS, SEGS - 2), 0, remainder[:, None] + 1)
    cut_points = jnp.sort(cut_points, axis=1)
    boundaries = jnp.concatenate([jnp.zeros((GROUPS, 1), jnp.int32), cut_points, remainder[:, None]], axis=1)
    doc_lengths = boundaries[:, 1:] - boundaries[:, :-1]
    return jnp.concatenate([longest[:, None], doc_lengths], axis=1).astype(jnp.int32)


def draw_vectors(key, part):
    key = jax.random.fold_in(key, 23)
    key_gain, key_shift = jax.random.split(key)
    row_ids = jnp.arange(6)[:, None]
    gain_rows = jax.random.uniform(key_gain, (6, D), jnp.float32, 0.5, 1.5)
    shifts = jnp.clip(0.5 * jax.random.normal(key_shift, (6, D), jnp.float32), -2.0, 2.0)
    is_gain = (row_ids == 0) | (row_ids == 3)
    return jnp.where(is_gain, gain_rows, shifts).astype(jnp.float32)


def levels(own_key, shape, cuts, least, top_value):
    level, own = 1.0, jax.random.fold_in(own_key, 6)
    for dim, parts in cuts:
        draws = jnp.exp(jax.random.uniform(jax.random.fold_in(own, dim), (parts,), jnp.float32, least / len(cuts), top_value / len(cuts)))
        level = level * jnp.repeat(draws, shape[dim] // parts).reshape([-1 if axis == dim else 1 for axis in range(len(shape))])
    return level


def gaussian(rng, extent, deviation, bound, cuts=(), kind=jnp.bfloat16):
    values = jax.random.normal(rng, extent, jnp.float32) * deviation
    if len(cuts) > 0:
        values = levels(rng, extent, cuts, -0.22, 0.18) * values
    return jnp.clip(values, min=-bound, max=bound).astype(kind)


def setup_inputs(seed: int = 0) -> dict:
    keys = jax.random.split(jax.random.key(seed), 11)
    tokens = gaussian(keys[0], (TOKENS, D), 1.0, 6.0, ((0, 32),))
    cotangent = gaussian(keys[1], (TOKENS, D), 1.0, 6.0, ((0, 32),))
    seg_lengths = draw_seg_lengths(jax.random.fold_in(keys[10], 71), 0)
    vectors = draw_vectors(jax.random.fold_in(keys[10], 71), 0)
    w_qkv = gaussian(keys[4], (D, 3, D), D ** -0.5, 0.1875, ((0, 8), (2, 4)))
    qv_bias = gaussian(keys[5], (2, HEADS, HD), 0.5, 3.0, ((1, 4), (2, 8)), jnp.float32)
    w_out = gaussian(keys[6], (D, D), (D // 8) ** -0.5, 0.5, ((0, 4), (1, 8)))
    w_up = gaussian(keys[7], (D, FF), D ** -0.5, 0.1875, ((0, 8), (1, 4)))
    up_bias = gaussian(keys[8], (HEADS, FF // HEADS), 0.5, 3.0, ((0, 4), (1, 8)), jnp.float32)
    w_down = gaussian(keys[9], (FF, D), (FF // 2) ** -0.5, 0.125, ((0, 4), (1, 8)))
    return dict(tokens=tokens, cotangent=cotangent, seg_lengths=seg_lengths, vectors=vectors, w_qkv=w_qkv, qv_bias=qv_bias, w_out=w_out, w_up=w_up, up_bias=up_bias, w_down=w_down)


@jax.custom_vjp
def low(v):
    return lax.optimization_barrier(v.astype(jnp.bfloat16)).astype(jnp.float32)

@jax.custom_vjp
def low_back(v):
    return v

def low_keep(v):
    return (low(v), None)

def low_pass(kept, grad):
    return (grad,)

def back_keep(v):
    return (v, None)

def back_low(kept, grad):
    return (low(grad),)
low.defvjp(low_keep, low_pass)
low_back.defvjp(back_keep, back_low)
epsilon = 1e-05
masked_score = -1e+30

def layer_norm(values, gain_vec, shift_vec):
    center = values - lax.optimization_barrier(jnp.mean(values, axis=-1, keepdims=True))
    spread = lax.optimization_barrier(jnp.mean(center * center, axis=-1, keepdims=True))
    return center * lax.rsqrt(spread + epsilon) * gain_vec + shift_vec

def doc_number(positions, lengths):
    doc_ends = jnp.cumsum(lengths)
    return lax.optimization_barrier(jnp.sum((positions[:, None] >= doc_ends[None, :]).astype(jnp.int32), axis=1))

def group_layer(inputs, lengths, params):
    vectors, w_qkv, qv_bias, w_out, w_up, up_bias, w_down = params
    highest = lax.Precision.HIGHEST
    normed = low(layer_norm(inputs, vectors[0], vectors[1]))
    projected = jnp.dot(normed, w_qkv.reshape(D, 3 * D), precision=highest).reshape(GROUP, 3, D)
    query_heads = low_back(low(projected[:, 0] + qv_bias[0].reshape(D))).reshape(GROUP, HEADS, HD)
    key_heads = low_back(low(projected[:, 1])).reshape(GROUP, HEADS, HD)
    value_heads = low_back(low(projected[:, 2] + qv_bias[1].reshape(D))).reshape(GROUP, HEADS, HD)
    positions = jnp.arange(GROUP, dtype=jnp.int32)
    doc_ids = doc_number(positions, lengths)
    allowed = (doc_ids[:, None] == doc_ids[None, :]) & (positions[None, :] <= positions[:, None])
    offset = (positions[:, None] - positions[None, :]).astype(jnp.float32)
    slopes = jnp.exp2(-8.0 * jnp.arange(1, HEADS + 1, dtype=jnp.float32) / HEADS)
    scores = jnp.einsum('qhd,khd->hqk', query_heads, key_heads, precision=highest) * HD ** (-0.5)
    scores = low_back(scores - slopes[:, None, None] * offset[None])
    scores = jnp.where(allowed[None], scores, masked_score)
    weights = low(jax.nn.softmax(scores, axis=-1))
    attended = jnp.einsum('hqk,khd->qhd', weights, value_heads, precision=highest).reshape(GROUP, D)
    attended = low_back(low(attended))
    branch = low_back(jnp.dot(attended, w_out, precision=highest))
    middle = inputs + branch + vectors[2]
    normed_two = low(layer_norm(middle, vectors[3], vectors[4]))
    pre_act = low_back(jnp.dot(normed_two, w_up, precision=highest) + up_bias.reshape(FF))
    activated = low(jax.nn.gelu(pre_act, approximate=True))
    branch_two = low_back(jnp.dot(activated, w_down, precision=highest))
    return middle + branch_two + vectors[5]

def reference(tokens, cotangent, seg_lengths, vectors, w_qkv, qv_bias, w_out, w_up, up_bias, w_down):
    params = tuple((item.astype(jnp.float32) for item in (vectors, w_qkv, qv_bias, w_out, w_up, up_bias, w_down)))
    inputs = tokens.astype(jnp.float32)

    def forward(layer_in, layer_params):
        grouped = layer_in.reshape(GROUPS, GROUP, D)
        step_fn = jax.checkpoint(lambda item_pair: group_layer(item_pair[0], item_pair[1], layer_params))
        return lax.map(step_fn, (grouped, seg_lengths)).reshape(TOKENS, D)
    result, pullback = jax.vjp(forward, inputs, params)
    grad_in, gradients = pullback(cotangent.astype(jnp.float32))
    return (result.astype(jnp.bfloat16), grad_in.astype(jnp.bfloat16), gradients[0], gradients[1], gradients[2], gradients[3], gradients[4], gradients[5], gradients[6])
```

```python
import jax
import jax.numpy as jnp
from jax import lax
from jax.experimental import pallas as pl
from jax.experimental.pallas import tpu as pltpu
from jax.sharding import PartitionSpec as P

epsilon = 1e-05
masked_score = -1e30


def layer_norm(values, gain_vec, shift_vec):
    center = values - jnp.mean(values, axis=-1, keepdims=True)
    spread = jnp.mean(center * center, axis=-1, keepdims=True)
    return center * lax.rsqrt(spread + epsilon) * gain_vec + shift_vec


def gelu_tanh(values):
    return jax.nn.gelu(values, approximate=True)


def doc_number(positions, lengths):
    doc_ends = jnp.cumsum(lengths)
    return jnp.sum((positions[:, None] >= doc_ends[None, :]).astype(jnp.int32), axis=1)


def block_scores(query_block, key_heads, first_row, slopes, lengths):
    block_size = query_block.shape[0]
    group_size = key_heads.shape[0]
    score_scale = query_block.shape[-1] ** (-0.5)
    scores = (
        jnp.einsum("qhd,khd->hqk", query_block, key_heads, preferred_element_type=jnp.float32)
        * score_scale
    )
    query_pos = first_row + jnp.arange(block_size, dtype=jnp.int32)
    key_pos = jnp.arange(group_size, dtype=jnp.int32)
    offset = (query_pos[:, None] - key_pos[None, :]).astype(jnp.float32)
    scores = scores - slopes[:, None, None] * offset[None]
    same_doc = doc_number(query_pos, lengths)[:, None] == doc_number(key_pos, lengths)[None, :]
    allowed = same_doc & (key_pos[None, :] <= query_pos[:, None])
    return jnp.where(allowed[None], scores, masked_score)


def on_device(
    tokens, cotangent, seg_lengths, vectors, w_qkv, qv_bias, w_out, w_up, up_bias, w_down
):
    model_width = tokens.shape[1]
    tensor_count = lax.axis_size("tensor")
    lengths = seg_lengths[0]
    gathered = (
        lax.all_gather(w_qkv, "dp", axis=0, tiled=True),
        lax.all_gather(qv_bias.astype(jnp.bfloat16), "dp", axis=2, tiled=True).astype(
            qv_bias.dtype
        ),
        lax.all_gather(w_out, "dp", axis=1, tiled=True),
        lax.all_gather(w_up, "dp", axis=0, tiled=True),
        lax.all_gather(up_bias.astype(jnp.bfloat16), "dp", axis=1, tiled=True).astype(
            up_bias.dtype
        ),
        lax.all_gather(w_down, "dp", axis=1, tiled=True),
        lax.all_gather(vectors.astype(jnp.bfloat16), "dp", axis=1, tiled=True).astype(
            vectors.dtype
        ),
    )
    qkv_full, bias_full, out_full, up_full, upbias_full, down_full, vec_full = gathered
    local_width = qkv_full.shape[2]
    heads_local = bias_full.shape[1]
    head_size = bias_full.shape[2]
    hidden_local = up_full.shape[1]
    head_ids = lax.axis_index("tensor") * heads_local + jnp.arange(heads_local, dtype=jnp.int32)
    slopes = jnp.exp2(-8.0 * (head_ids + 1).astype(jnp.float32) / (heads_local * tensor_count))
    inputs = tokens.astype(jnp.float32)
    normed_one = layer_norm(inputs, vec_full[0], vec_full[1]).astype(jnp.bfloat16)
    group_one = lax.all_gather(normed_one, "tensor", axis=0, tiled=True)
    group_size = group_one.shape[0]
    projected = jnp.dot(
        group_one,
        qkv_full.reshape(model_width, 3 * local_width),
        preferred_element_type=jnp.float32,
    )
    projected = projected.reshape(group_size, 3, local_width)
    head_shape = (group_size, heads_local, head_size)
    query_heads = (
        (projected[:, 0] + bias_full[0].reshape(local_width))
        .astype(jnp.bfloat16)
        .reshape(head_shape)
    )
    key_heads = projected[:, 1].astype(jnp.bfloat16).reshape(head_shape)
    value_heads = (
        (projected[:, 2] + bias_full[1].reshape(local_width))
        .astype(jnp.bfloat16)
        .reshape(head_shape)
    )
    block_index = 0
    first_row = block_index * group_size
    scores = block_scores(query_heads, key_heads, first_row, slopes, lengths)
    row_max = jnp.max(scores, axis=-1, keepdims=True)
    exponent = jnp.exp(scores - row_max)
    row_sum = jnp.sum(exponent, axis=-1, keepdims=True)
    weights = (exponent / row_sum).astype(jnp.bfloat16)
    out_blocks = jnp.einsum(
        "hqk,khd->qhd", weights, value_heads, preferred_element_type=jnp.float32
    )
    lse_blocks = (row_max + jnp.log(row_sum))[..., 0]
    attended = out_blocks.reshape(group_size, local_width).astype(jnp.bfloat16)
    branch_attn = lax.psum_scatter(
        jnp.dot(attended, out_full, preferred_element_type=jnp.float32).astype(jnp.bfloat16),
        "tensor",
        scatter_dimension=0,
        tiled=True,
    ).astype(jnp.float32)
    middle = inputs + branch_attn + vec_full[2]
    normed_two = layer_norm(middle, vec_full[3], vec_full[4]).astype(jnp.bfloat16)
    group_two = lax.all_gather(normed_two, "tensor", axis=0, tiled=True)
    pre_act = jnp.dot(group_two, up_full, preferred_element_type=jnp.float32) + upbias_full.reshape(
        hidden_local
    )
    activated = gelu_tanh(pre_act).astype(jnp.bfloat16)
    branch_mlp = lax.psum_scatter(
        jnp.dot(activated, down_full, preferred_element_type=jnp.float32).astype(jnp.bfloat16),
        "tensor",
        scatter_dimension=0,
        tiled=True,
    ).astype(jnp.float32)
    output = (middle + branch_mlp + vec_full[5]).astype(jnp.bfloat16)
    qkv_back, out_back, up_back, down_back = (
        lax.all_gather(w_qkv, "dp", axis=0, tiled=True),
        lax.all_gather(w_out, "dp", axis=1, tiled=True),
        lax.all_gather(w_up, "dp", axis=0, tiled=True),
        lax.all_gather(w_down, "dp", axis=1, tiled=True),
    )
    grad_output = cotangent.astype(jnp.float32)
    grad_mlp = grad_output.astype(jnp.bfloat16)
    shard_rows = lax.all_gather(grad_mlp, "tensor", axis=0, tiled=True)
    used_rows = activated
    grad_weight = lax.dot_general(
        used_rows, shard_rows, (((0,), (0,)), ((), ())), preferred_element_type=jnp.float32
    )
    partial_value = lax.dot_general(
        shard_rows, down_back, (((1,), (1,)), ((), ())), preferred_element_type=jnp.float32
    )
    grad_down = grad_weight
    grad_act = partial_value
    _, gelu_back = jax.vjp(gelu_tanh, pre_act)
    grad_pre = gelu_back(grad_act)[0].astype(jnp.bfloat16)
    grad_upbias = jnp.sum(grad_pre.astype(jnp.float32), axis=0).reshape(upbias_full.shape)
    grad_up = lax.dot_general(
        group_two, grad_pre, (((0,), (0,)), ((), ())), preferred_element_type=jnp.float32
    )
    used_rows = grad_pre
    grad_normed_two = lax.psum_scatter(
        lax.dot_general(
            used_rows, up_back, (((1,), (1,)), ((), ())), preferred_element_type=jnp.float32
        ).astype(jnp.bfloat16),
        "tensor",
        scatter_dimension=0,
        tiled=True,
    ).astype(jnp.float32)
    _, norm_two_back = jax.vjp(layer_norm, middle, vec_full[3], vec_full[4])
    grad_mid_norm, grad_gain_two, grad_shift_two = norm_two_back(grad_normed_two)
    grad_middle = grad_output + grad_mid_norm
    grad_attn = grad_middle.astype(jnp.bfloat16)
    shard_rows = lax.all_gather(grad_attn, "tensor", axis=0, tiled=True)
    used_rows = attended
    grad_weight = lax.dot_general(
        used_rows, shard_rows, (((0,), (0,)), ((), ())), preferred_element_type=jnp.float32
    )
    partial_value = lax.dot_general(
        shard_rows, out_back, (((1,), (1,)), ((), ())), preferred_element_type=jnp.float32
    )
    grad_heads = partial_value.astype(jnp.bfloat16).reshape(head_shape)
    score_scale = head_size ** (-0.5)
    block_index = 0
    first_row = block_index * group_size
    scores = block_scores(query_heads, key_heads, first_row, slopes, lengths)
    probs = jnp.exp(scores - lse_blocks[:, first_row : first_row + group_size, None])
    weights = probs.astype(jnp.bfloat16)
    grad_probs = jnp.einsum(
        "qhd,khd->hqk", grad_heads, value_heads, preferred_element_type=jnp.float32
    )
    row_term = jnp.sum(probs * grad_probs, axis=-1, keepdims=True)
    grad_scores = (probs * (grad_probs - row_term)).astype(jnp.bfloat16)
    query_parts = (
        jnp.einsum("hqk,khd->qhd", grad_scores, key_heads, preferred_element_type=jnp.float32)
        * score_scale
    )
    grad_keys = (
        jnp.einsum("hqk,qhd->khd", grad_scores, query_heads, preferred_element_type=jnp.float32)
        * score_scale
    )
    grad_values = jnp.einsum(
        "hqk,qhd->khd", weights, grad_heads, preferred_element_type=jnp.float32
    )
    grad_query = query_parts.reshape(group_size, local_width).astype(jnp.bfloat16)
    grad_key = grad_keys.reshape(group_size, local_width).astype(jnp.bfloat16)
    grad_value = grad_values.reshape(group_size, local_width).astype(jnp.bfloat16)
    grad_proj = jnp.stack([grad_query, grad_key, grad_value], axis=1)
    grad_qvbias = jnp.stack(
        [
            jnp.sum(grad_query.astype(jnp.float32), axis=0),
            jnp.sum(grad_value.astype(jnp.float32), axis=0),
        ]
    ).reshape(bias_full.shape)
    grad_qkv = lax.dot_general(
        group_one, grad_proj, (((0,), (0,)), ((), ())), preferred_element_type=jnp.float32
    )
    used_rows = grad_proj
    grad_normed_one = lax.psum_scatter(
        lax.dot_general(
            used_rows, qkv_back, (((1, 2), (1, 2)), ((), ())), preferred_element_type=jnp.float32
        ).astype(jnp.bfloat16),
        "tensor",
        scatter_dimension=0,
        tiled=True,
    ).astype(jnp.float32)
    _, norm_one_back = jax.vjp(layer_norm, inputs, vec_full[0], vec_full[1])
    grad_in_norm, grad_gain_one, grad_shift_one = norm_one_back(grad_normed_one)
    grad_tokens = (grad_middle + grad_in_norm).astype(jnp.bfloat16)
    grad_vecs = jnp.stack(
        [
            grad_gain_one,
            grad_shift_one,
            jnp.sum(grad_middle, axis=0),
            grad_gain_two,
            grad_shift_two,
            jnp.sum(grad_output, axis=0),
        ]
    )
    sent_qkv, sent_qvbias, sent_out, sent_up, sent_upbias, sent_down, sent_vecs = (
        lax.psum_scatter(grad_qkv, "dp", scatter_dimension=0, tiled=True),
        lax.psum_scatter(grad_qvbias, "dp", scatter_dimension=2, tiled=True),
        lax.psum_scatter(grad_weight, "dp", scatter_dimension=1, tiled=True),
        lax.psum_scatter(grad_up, "dp", scatter_dimension=0, tiled=True),
        lax.psum_scatter(grad_upbias, "dp", scatter_dimension=1, tiled=True),
        lax.psum_scatter(grad_down, "dp", scatter_dimension=1, tiled=True),
        lax.psum_scatter(grad_vecs, "dp", scatter_dimension=1, tiled=True),
    )
    sent_vecs = lax.psum(sent_vecs, "tensor")
    return (
        output,
        grad_tokens,
        sent_vecs,
        sent_qkv,
        sent_qvbias,
        sent_out,
        sent_up,
        sent_upbias,
        sent_down,
    )


Z_COUNT, Y_COUNT, T_COUNT = 4, 2, 4
MESH_ID = pl.DeviceIdType.MESH
ANYWHERE = pl.BlockSpec(memory_space=pl.ANY)
IN_VMEM = pl.BlockSpec(memory_space=pltpu.VMEM)


class Place:
    def __init__(self):
        dp = lax.axis_index("dp")
        self.t = lax.axis_index("tensor")
        self.z = dp // Y_COUNT
        self.y = dp % Y_COUNT
        self.other_y = 1 - self.y
        self.dp = dp

    def owner(self, z_index, y_index):
        return z_index * Y_COUNT + y_index

    def z_next(self, step):
        return lax.rem(self.z + step, Z_COUNT)

    def z_prev(self, step):
        return lax.rem(self.z + Z_COUNT - step, Z_COUNT)

    def z_peer(self, step):
        return (self.owner(self.z_next(step), self.y), self.t)

    def y_peer(self):
        return (self.owner(self.z, self.other_y), self.t)

    def t_next(self, step):
        return lax.rem(self.t + step, T_COUNT)

    def t_peer(self, step):
        return (self.dp, self.t_next(step))

    def barrier(self):
        sem = pltpu.get_barrier_semaphore()
        peers = [self.z_peer(k) for k in range(1, Z_COUNT)]
        peers += [self.y_peer()]
        peers += [self.t_peer(k) for k in range(1, T_COUNT)]
        for peer in peers:
            pl.semaphore_signal(sem, inc=1, device_id=peer, device_id_type=MESH_ID)
        pl.semaphore_wait(sem, len(peers))


def block_of(ref, owner, size, axis):
    start = pl.multiple_of(owner * size, size)
    if axis == 0:
        return ref.at[pl.ds(start, size), :]
    return ref.at[:, pl.ds(start, size)]


def remote(src, dst, send_sem, recv_sem, peer):
    return pltpu.make_async_remote_copy(
        src_ref=src,
        dst_ref=dst,
        send_sem=send_sem,
        recv_sem=recv_sem,
        device_id=peer,
        device_id_type=MESH_ID,
    )


class DpGather:
    def __init__(self, here, shard, full, axis, sems):
        self.here, self.shard, self.full, self.axis = here, shard, full, axis
        self.send, self.recv, self.own = sems
        self.size = shard.shape[axis]
        self.flights = []

    def slot(self, owner):
        return block_of(self.full, owner, self.size, self.axis)

    def start(self):
        here = self.here
        mine = self.slot(here.dp)
        self.local = pltpu.make_async_copy(self.shard, mine, self.own)
        self.local.start()
        self.z_flights = []
        self.y_flights = [remote(self.shard, mine, self.send.at[3], self.recv.at[3], here.y_peer())]
        self.y_flights[0].start()
        for k in range(1, Z_COUNT):
            flight = remote(self.shard, mine, self.send.at[k - 1], self.recv.at[k - 1], here.z_peer(k))
            flight.start()
            self.z_flights.append(flight)

    def forward(self):
        here = self.here
        for k in range(1, Z_COUNT):
            self.z_flights[k - 1].wait_recv()
            held = self.slot(here.owner(here.z_prev(k), here.y))
            flight = remote(held, held, self.send.at[3 + k], self.recv.at[3 + k], here.y_peer())
            flight.start()
            self.y_flights.append(flight)

    def finish(self):
        for flight in self.y_flights:
            flight.wait_recv()
        for flight in self.z_flights + self.y_flights:
            flight.wait_send()
        self.local.wait()


class DpScatter:
    def __init__(self, here, part, total, axis, y_buf, z_out, z_in, sems):
        self.here, self.part, self.total, self.axis = here, part, total, axis
        self.y_buf, self.z_out, self.z_in = y_buf, z_out, z_in
        self.send, self.recv = sems
        self.size = total.shape[axis]

    def slot(self, owner):
        return block_of(self.part, owner, self.size, self.axis)

    def start(self):
        here = self.here
        self.y_flights = {}
        for k in (1, 2, 3, 0):
            src = self.slot(here.owner(here.z_next(k), here.other_y))
            flight = remote(src, self.y_buf.at[k], self.send.at[k], self.recv.at[k], here.y_peer())
            flight.start()
            self.y_flights[k] = flight

    def middle(self):
        here = self.here
        self.z_flights = []
        for k in range(1, Z_COUNT):
            self.y_flights[k].wait_recv()
            own = self.slot(here.owner(here.z_next(k), here.y))[...]
            both = own.astype(jnp.float32) + self.y_buf[k].astype(jnp.float32)
            self.z_out[k - 1] = both.astype(self.z_out.dtype)
            flight = remote(
                self.z_out.at[k - 1],
                self.z_in.at[k - 1],
                self.send.at[3 + k],
                self.recv.at[3 + k],
                here.z_peer(k),
            )
            flight.start()
            self.z_flights.append(flight)

    def finish(self):
        self.y_flights[0].wait_recv()
        own = self.slot(self.here.dp)[...].astype(jnp.float32)
        acc = own + self.y_buf[0].astype(jnp.float32)
        for k in range(1, Z_COUNT):
            self.z_flights[k - 1].wait_recv()
            acc = acc + self.z_in[k - 1].astype(jnp.float32)
        self.total[...] = acc
        for flight in list(self.y_flights.values()) + self.z_flights:
            flight.wait_send()


class TensorGather:
    def __init__(self, here, full, rows, send, recv):
        self.here, self.full, self.rows = here, full, rows
        self.send, self.recv = send, recv

    def start(self, src=None):
        here = self.here
        mine = block_of(self.full, here.t, self.rows, 0)
        self.flights = []
        for k in (2, 3, 1):
            flight = remote(
                mine if src is None else src,
                mine,
                self.send.at[k - 1],
                self.recv.at[k - 1],
                here.t_peer(k),
            )
            flight.start()
            self.flights.append(flight)

    def finish(self):
        for flight in self.flights:
            flight.wait_recv()
        for flight in self.flights:
            flight.wait_send()


class TensorScatter:
    def __init__(self, here, part, buf, send, recv):
        self.here, self.part, self.buf = here, part, buf
        self.send, self.recv = send, recv
        self.rows = buf.shape[1]

    def start(self):
        here = self.here
        self.flights = []
        for k in (2, 3, 1):
            flight = remote(
                block_of(self.part, here.t_next(k), self.rows, 0),
                self.buf.at[k - 1],
                self.send.at[k - 1],
                self.recv.at[k - 1],
                here.t_peer(k),
            )
            flight.start()
            self.flights.append(flight)

    def total(self):
        for flight in self.flights:
            flight.wait_recv()
        acc = block_of(self.part, self.here.t, self.rows, 0)[...].astype(jnp.float32)
        for k in range(T_COUNT - 1):
            acc = acc + self.buf[k].astype(jnp.float32)
        return acc

    def finish(self):
        for flight in self.flights:
            flight.wait_send()


DMA = pltpu.SemaphoreType.DMA
gather_sems = [DMA((7,)), DMA((7,)), DMA]
pair_sems = [DMA((7,)), DMA((7,))]
tensor_sems = [DMA((3,)), DMA((3,))]


def scatter_scratch(block, dtype):
    return [
        pltpu.VMEM((4,) + block, dtype),
        pltpu.VMEM((3,) + block, dtype),
        pltpu.VMEM((3,) + block, dtype),
    ] + pair_sems


def call(kernel, name, outs, in_specs, out_specs, scratch, collective_id):
    return pl.pallas_call(
        kernel,
        name=name,
        out_shape=outs,
        in_specs=in_specs,
        out_specs=out_specs,
        scratch_shapes=scratch,
        compiler_params=pltpu.CompilerParams(
            collective_id=collective_id,
            has_side_effects=True,
            vmem_limit_bytes=44 * 1024 * 1024,
        ),
    )


def gather_kernel(
    tok, cot, small, qkv, out, up, tok_full, cot_full, small_full, qkv_full, out_full, up_full, *sems
):
    here = Place()
    here.barrier()
    rows = tok.shape[0]
    shards = (
        (small, small_full, 0),
        (qkv, qkv_full, 0),
        (out, out_full, 1),
        (up, up_full, 0),
    )
    gathers = [
        DpGather(here, shard, full, axis, sems[3 * i : 3 * i + 3])
        for i, (shard, full, axis) in enumerate(shards)
    ]
    rest = sems[3 * len(shards) :]
    across = []
    for i, (own, full) in enumerate(((tok, tok_full), (cot, cot_full))):
        local = pltpu.make_async_copy(own, block_of(full, here.t, rows, 0), rest[4 + i])
        local.start()
        moving = TensorGather(here, full, rows, rest[2 * i], rest[2 * i + 1])
        moving.start(own)
        across.append((local, moving))
    for item in gathers:
        item.start()
    for item in gathers:
        item.forward()
    for item in gathers:
        item.finish()
    for local, moving in across:
        moving.finish()
        local.wait()


def normalize(values):
    center = values - jnp.mean(values, axis=-1, keepdims=True)
    scale = lax.rsqrt(jnp.mean(center * center, axis=-1, keepdims=True) + epsilon)
    return center * scale, scale


def middle_kernel(
    part, tok, vec, down, mid, normed_full, down_full, buf, g_send, g_recv, g_own, s_send, s_recv, a_send, a_recv
):
    here = Place()
    here.barrier()
    scatter = TensorScatter(here, part, buf, s_send, s_recv)
    scatter.start()
    weights = DpGather(here, down, down_full, 1, (g_send, g_recv, g_own))
    weights.start()
    rows = tok.shape[0]
    middle = tok[...].astype(jnp.float32) + scatter.total() + vec[2:3]
    mid[...] = middle
    hat, _ = normalize(middle)
    block_of(normed_full, here.t, rows, 0)[...] = (hat * vec[3:4] + vec[4:5]).astype(jnp.bfloat16)
    spread = TensorGather(here, normed_full, rows, a_send, a_recv)
    spread.start()
    weights.forward()
    spread.finish()
    weights.finish()
    scatter.finish()


def norm_back(grad, values, gain):
    hat, scale = normalize(values)
    e = grad * gain
    inner = scale * (
        e - jnp.mean(e, axis=-1, keepdims=True) - hat * jnp.mean(e * hat, axis=-1, keepdims=True)
    )
    gain_grad = jnp.sum(grad * hat, axis=0, keepdims=True)
    shift_grad = jnp.sum(grad, axis=0, keepdims=True)
    return inner, gain_grad, shift_grad


def back_kernel(
    part_mlp, part_norm, mid, cot, vec, grad_down, result, grad_mid, attn_full, sums, total_down,
    buf_norm, buf_mlp, y_buf, z_out, z_in, d_send, d_recv, n_send, n_recv, m_send, m_recv, a_send, a_recv
):
    here = Place()
    here.barrier()
    rows = mid.shape[0]
    first = TensorScatter(here, part_norm, buf_norm, n_send, n_recv)
    first.start()
    second = TensorScatter(here, part_mlp, buf_mlp, m_send, m_recv)
    second.start()
    down = DpScatter(here, grad_down, total_down, 1, y_buf, z_out, z_in, (d_send, d_recv))
    down.start()
    grad_out = cot[...].astype(jnp.float32)
    inner, gain_grad, shift_grad = norm_back(first.total(), mid[...], vec[3:4])
    grad = grad_out + inner
    grad_mid[...] = grad
    block_of(attn_full, here.t, rows, 0)[...] = grad.astype(jnp.bfloat16)
    spread = TensorGather(here, attn_full, rows, a_send, a_recv)
    spread.start()
    zero = jnp.zeros_like(gain_grad)
    sums[0:1] = zero
    sums[1:2] = zero
    sums[2:3] = jnp.sum(grad, axis=0, keepdims=True)
    sums[3:4] = gain_grad
    sums[4:5] = shift_grad
    sums[5:6] = jnp.sum(grad_out, axis=0, keepdims=True)
    sums[6:7] = zero
    sums[7:8] = zero
    result[...] = (mid[...] + second.total() + vec[5:6]).astype(jnp.bfloat16)
    down.middle()
    spread.finish()
    down.finish()
    first.finish()
    second.finish()


def last_kernel(
    part, tok, grad_mid, vec, sums, bias_rows, grad_out, grad_up, grad_qkv,
    grad_tok, total_small, total_out, total_up, total_qkv,
    buf, small_part, small_mine, small_sum, small_buf, t_send, t_recv, v_send, v_recv, *scratch
):
    here = Place()
    here.barrier()
    scatter = TensorScatter(here, part, buf, t_send, t_recv)
    scatter.start()
    plan = ((grad_out, total_out, 1), (grad_up, total_up, 0), (grad_qkv, total_qkv, 0))
    big = []
    for i, (ref, total, axis) in enumerate(plan):
        group = scratch[5 * i : 5 * i + 5]
        item = DpScatter(here, ref, total, axis, *group[:3], group[3:])
        item.start()
        big.append(item)
    inner, gain_grad, shift_grad = norm_back(
        scatter.total(), tok[...].astype(jnp.float32), vec[0:1]
    )
    grad_tok[...] = (grad_mid[...] + inner).astype(jnp.bfloat16)
    width = total_small.shape[1]
    for d in range(Z_COUNT * Y_COUNT):
        cols = slice(d * width, (d + 1) * width)
        small_part[8 * d : 8 * d + 8] = sums[:, cols] + bias_rows[8 * d : 8 * d + 8]
        small_part[8 * d : 8 * d + 1] = gain_grad[:, cols]
        small_part[8 * d + 1 : 8 * d + 2] = shift_grad[:, cols]
    group = scratch[15:20]
    small = DpScatter(here, small_part, small_mine, 0, *group[:3], group[3:])
    small.start()
    big[0].middle()
    small.middle()
    big[1].middle()
    big[2].middle()
    small.finish()
    small_sum[...] = small_mine[...]
    flights = []
    for k in range(1, T_COUNT):
        flight = remote(
            small_sum, small_buf.at[k - 1], v_send.at[k - 1], v_recv.at[k - 1], here.t_peer(k)
        )
        flight.start()
        flights.append(flight)
    for item in big:
        item.finish()
    for flight in flights:
        flight.wait_recv()
    everyone = small_mine[...] + small_buf[0] + small_buf[1] + small_buf[2]
    row = lax.broadcasted_iota(jnp.int32, everyone.shape, 0)
    total_small[...] = jnp.where(row < 6, everyone, small_mine[...])
    for flight in flights:
        flight.wait_send()
    scatter.finish()


def on_device_direct(
    tokens, cotangent, seg_lengths, vectors, w_qkv, qv_bias, w_out, w_up, up_bias, w_down
):
    bf16, f32 = jnp.bfloat16, jnp.float32
    rows, width = tokens.shape
    heads, head_part = qv_bias.shape[1], qv_bias.shape[2]
    dp, cols = Z_COUNT * Y_COUNT, vectors.shape[1]
    head_size = head_part * dp
    group_size = rows * T_COUNT
    local_width = w_qkv.shape[2]
    hidden = w_up.shape[1]
    up_part = up_bias.shape[1]
    lengths = seg_lengths[0]
    shape = jax.ShapeDtypeStruct
    qkv_wide = 3 * local_width
    qv_row = jnp.pad(qv_bias.reshape(1, -1), ((0, 0), (0, cols - qv_bias.size)))
    small = jnp.concatenate(
        [vectors, qv_row, up_bias.reshape(1, cols), jnp.zeros((8, cols), f32)]
    ).astype(bf16)
    tok_full, cot_full, small_full, qkv_full, out_full, up_full = call(
        gather_kernel,
        "gather_inputs",
        [
            shape((group_size, width), bf16),
            shape((group_size, width), bf16),
            shape((dp * 16, cols), bf16),
            shape((width, qkv_wide), bf16),
            shape((local_width, width), bf16),
            shape((width, hidden), bf16),
        ],
        [ANYWHERE] * 6,
        [ANYWHERE] * 6,
        gather_sems * 4 + tensor_sems * 2 + [DMA, DMA],
        1,
    )(tokens, cotangent, small, w_qkv.reshape(-1, qkv_wide), w_out, w_up)
    small_full = small_full.reshape(dp, 16, cols).astype(f32)
    vec_full = small_full[:, :8].transpose(1, 0, 2).reshape(8, width)
    bias_full = (
        small_full[:, 6, : qv_bias.size]
        .reshape(dp, 2, heads, head_part)
        .transpose(1, 2, 0, 3)
        .reshape(2, local_width)
    )
    upbias_full = small_full[:, 7].reshape(dp, heads, up_part).transpose(1, 0, 2).reshape(hidden)

    head_ids = lax.axis_index("tensor") * heads + jnp.arange(heads, dtype=jnp.int32)
    slopes = jnp.exp2(-8.0 * (head_ids + 1).astype(f32) / (heads * T_COUNT))
    group_one = layer_norm(tok_full.astype(f32), vec_full[0], vec_full[1]).astype(bf16)
    projected = jnp.dot(group_one, qkv_full, preferred_element_type=f32)
    projected = projected.reshape(group_size, 3, local_width)
    head_shape = (group_size, heads, head_size)
    query_heads = (projected[:, 0] + bias_full[0]).astype(bf16).reshape(head_shape)
    key_heads = projected[:, 1].astype(bf16).reshape(head_shape)
    value_heads = (projected[:, 2] + bias_full[1]).astype(bf16).reshape(head_shape)
    scores = block_scores(query_heads, key_heads, 0, slopes, lengths)
    row_max = jnp.max(scores, axis=-1, keepdims=True)
    exponent = jnp.exp(scores - row_max)
    row_sum = jnp.sum(exponent, axis=-1, keepdims=True)
    probs = exponent / row_sum
    weights = probs.astype(bf16)
    attended = (
        jnp.einsum("hqk,khd->qhd", weights, value_heads, preferred_element_type=f32)
        .reshape(group_size, local_width)
        .astype(bf16)
    )
    part_attn = jnp.dot(attended, out_full, preferred_element_type=f32).astype(bf16)

    middle, group_two, down_full = call(
        middle_kernel,
        "middle",
        [
            shape((rows, width), f32),
            shape((group_size, width), bf16),
            shape((hidden, width), bf16),
        ],
        [IN_VMEM, IN_VMEM, IN_VMEM, ANYWHERE],
        [IN_VMEM, IN_VMEM, ANYWHERE],
        [pltpu.VMEM((3, rows, width), bf16)] + gather_sems + tensor_sems * 2,
        2,
    )(part_attn, tokens, vec_full, w_down)

    contract_rows = (((0,), (0,)), ((), ()))
    contract_cols = (((1,), (1,)), ((), ()))
    pre_act = jnp.dot(group_two, up_full, preferred_element_type=f32) + upbias_full
    activated, gelu_back = jax.vjp(gelu_tanh, pre_act)
    activated = activated.astype(bf16)
    part_mlp = jnp.dot(activated, down_full, preferred_element_type=f32).astype(bf16)
    grad_act = lax.dot_general(cot_full, down_full, contract_cols, preferred_element_type=f32)
    grad_pre = gelu_back(grad_act)[0].astype(bf16)
    part_norm = lax.dot_general(
        grad_pre, up_full, contract_cols, preferred_element_type=f32
    ).astype(bf16)
    grad_down = lax.dot_general(
        activated, cot_full, contract_rows, preferred_element_type=f32
    ).astype(bf16)
    grad_up = lax.dot_general(
        group_two, grad_pre, contract_rows, preferred_element_type=f32
    ).astype(bf16)
    grad_upbias = jnp.sum(grad_pre.astype(f32), axis=0)

    output, grad_middle, attn_full, sums, total_down = call(
        back_kernel,
        "back",
        [
            shape((rows, width), bf16),
            shape((rows, width), f32),
            shape((group_size, width), bf16),
            shape((8, width), f32),
            shape((hidden, cols), f32),
        ],
        [IN_VMEM] * 6,
        [IN_VMEM] * 5,
        [pltpu.VMEM((3, rows, width), bf16)] * 2
        + scatter_scratch((hidden, cols), bf16)
        + tensor_sems * 3,
        3,
    )(part_mlp, part_norm, middle, cotangent, vec_full, grad_down)

    grad_out = lax.dot_general(
        attended, attn_full, contract_rows, preferred_element_type=f32
    ).astype(bf16)
    grad_heads = (
        lax.dot_general(attn_full, out_full, contract_cols, preferred_element_type=f32)
        .astype(bf16)
        .reshape(head_shape)
    )
    score_scale = head_size ** (-0.5)
    grad_probs = jnp.einsum("qhd,khd->hqk", grad_heads, value_heads, preferred_element_type=f32)
    row_term = jnp.sum(probs * grad_probs, axis=-1, keepdims=True)
    grad_scores = (probs * (grad_probs - row_term)).astype(bf16)
    grad_query = (
        jnp.einsum("hqk,khd->qhd", grad_scores, key_heads, preferred_element_type=f32) * score_scale
    )
    grad_keys = (
        jnp.einsum("hqk,qhd->khd", grad_scores, query_heads, preferred_element_type=f32)
        * score_scale
    )
    grad_values = jnp.einsum("hqk,qhd->khd", weights, grad_heads, preferred_element_type=f32)
    grad_proj = jnp.concatenate(
        [item.reshape(group_size, local_width).astype(bf16) for item in (grad_query, grad_keys, grad_values)],
        axis=1,
    )
    bias_sums = jnp.sum(grad_proj.astype(f32), axis=0)
    grad_qvbias = jnp.stack([bias_sums[:local_width], bias_sums[2 * local_width :]])
    grad_qkv = lax.dot_general(
        group_one, grad_proj, contract_rows, preferred_element_type=f32
    ).astype(bf16)
    part_first = lax.dot_general(
        grad_proj, qkv_full, contract_cols, preferred_element_type=f32
    ).astype(bf16)
    qv_rows = (
        grad_qvbias.reshape(2, heads, dp, head_part).transpose(2, 0, 1, 3).reshape(dp, 1, qv_bias.size)
    )
    qv_rows = jnp.pad(qv_rows, ((0, 0), (0, 0), (0, cols - qv_bias.size)))
    up_rows = grad_upbias.reshape(heads, dp, up_part).transpose(1, 0, 2).reshape(dp, 1, cols)
    bias_rows = jnp.concatenate([jnp.zeros((dp, 6, cols), f32), qv_rows, up_rows], axis=1)
    bias_rows = bias_rows.reshape(dp * 8, cols)

    grad_tokens, total_small, total_out, total_up, total_qkv = call(
        last_kernel,
        "last",
        [
            shape((rows, width), bf16),
            shape((8, cols), f32),
            shape((local_width, cols), f32),
            shape((width // dp, hidden), f32),
            shape((width // dp, qkv_wide), f32),
        ],
        [IN_VMEM] * 9,
        [IN_VMEM] * 5,
        [
            pltpu.VMEM((3, rows, width), bf16),
            pltpu.VMEM((8 * dp, cols), f32),
            pltpu.VMEM((8, cols), f32),
            pltpu.VMEM((8, cols), f32),
            pltpu.VMEM((3, 8, cols), f32),
        ]
        + tensor_sems * 2
        + scatter_scratch((local_width, cols), bf16)
        + scatter_scratch((width // dp, hidden), bf16)
        + scatter_scratch((width // dp, qkv_wide), bf16)
        + scatter_scratch((8, cols), f32),
        4,
    )(part_first, tokens, grad_middle, vec_full, sums, bias_rows, grad_out, grad_up, grad_qkv)
    return (
        output,
        grad_tokens,
        total_small[:6],
        total_qkv.reshape(w_qkv.shape),
        total_small[6, : qv_bias.size].reshape(qv_bias.shape),
        total_out,
        total_up,
        total_small[7].reshape(up_bias.shape),
        total_down,
    )


def solution(mesh):
    direct = mesh.shape["dp"] == Z_COUNT * Y_COUNT and mesh.shape["tensor"] == T_COUNT
    return jax.shard_map(
        on_device_direct if direct else on_device,
        mesh=mesh,
        in_specs=(
            P(("dp", "tensor"), None),
            P(("dp", "tensor"), None),
            P("dp", None),
            P(None, "dp"),
            P("dp", None, "tensor"),
            P(None, "tensor", "dp"),
            P("tensor", "dp"),
            P("dp", "tensor"),
            P("tensor", "dp"),
            P("tensor", "dp"),
        ),
        out_specs=(
            P(("dp", "tensor"), None),
            P(("dp", "tensor"), None),
            P(None, "dp"),
            P("dp", None, "tensor"),
            P(None, "tensor", "dp"),
            P("tensor", "dp"),
            P("dp", "tensor"),
            P("tensor", "dp"),
            P("tensor", "dp"),
        ),
        check_vma=False,
    )
```

```python
import jax
import jax.numpy as jnp
from jax import lax
from jax.experimental import pallas as pl
from jax.experimental.pallas import tpu as pltpu
from jax.sharding import PartitionSpec as P

epsilon = 1e-05
masked_score = -1e30


def layer_norm(values, gain_vec, shift_vec):
    center = values - jnp.mean(values, axis=-1, keepdims=True)
    spread = jnp.mean(center * center, axis=-1, keepdims=True)
    return center * lax.rsqrt(spread + epsilon) * gain_vec + shift_vec


def gelu_tanh(values):
    return jax.nn.gelu(values, approximate=True)


def doc_number(positions, lengths):
    doc_ends = jnp.cumsum(lengths)
    return jnp.sum((positions[:, None] >= doc_ends[None, :]).astype(jnp.int32), axis=1)


def block_scores(query_block, key_heads, first_row, slopes, lengths):
    block_size = query_block.shape[0]
    group_size = key_heads.shape[0]
    score_scale = query_block.shape[-1] ** (-0.5)
    scores = (
        jnp.einsum("qhd,khd->hqk", query_block, key_heads, preferred_element_type=jnp.float32)
        * score_scale
    )
    query_pos = first_row + jnp.arange(block_size, dtype=jnp.int32)
    key_pos = jnp.arange(group_size, dtype=jnp.int32)
    offset = (query_pos[:, None] - key_pos[None, :]).astype(jnp.float32)
    scores = scores - slopes[:, None, None] * offset[None]
    same_doc = doc_number(query_pos, lengths)[:, None] == doc_number(key_pos, lengths)[None, :]
    allowed = same_doc & (key_pos[None, :] <= query_pos[:, None])
    return jnp.where(allowed[None], scores, masked_score)


def on_device(
    tokens, cotangent, seg_lengths, vectors, w_qkv, qv_bias, w_out, w_up, up_bias, w_down
):
    model_width = tokens.shape[1]
    tensor_count = lax.axis_size("tensor")
    lengths = seg_lengths[0]
    gathered = (
        lax.all_gather(w_qkv, "dp", axis=0, tiled=True),
        lax.all_gather(qv_bias.astype(jnp.bfloat16), "dp", axis=2, tiled=True).astype(
            qv_bias.dtype
        ),
        lax.all_gather(w_out, "dp", axis=1, tiled=True),
        lax.all_gather(w_up, "dp", axis=0, tiled=True),
        lax.all_gather(up_bias.astype(jnp.bfloat16), "dp", axis=1, tiled=True).astype(
            up_bias.dtype
        ),
        lax.all_gather(w_down, "dp", axis=1, tiled=True),
        lax.all_gather(vectors.astype(jnp.bfloat16), "dp", axis=1, tiled=True).astype(
            vectors.dtype
        ),
    )
    qkv_full, bias_full, out_full, up_full, upbias_full, down_full, vec_full = gathered
    local_width = qkv_full.shape[2]
    heads_local = bias_full.shape[1]
    head_size = bias_full.shape[2]
    hidden_local = up_full.shape[1]
    head_ids = lax.axis_index("tensor") * heads_local + jnp.arange(heads_local, dtype=jnp.int32)
    slopes = jnp.exp2(-8.0 * (head_ids + 1).astype(jnp.float32) / (heads_local * tensor_count))
    inputs = tokens.astype(jnp.float32)
    normed_one = layer_norm(inputs, vec_full[0], vec_full[1]).astype(jnp.bfloat16)
    group_one = lax.all_gather(normed_one, "tensor", axis=0, tiled=True)
    group_size = group_one.shape[0]
    projected = jnp.dot(
        group_one,
        qkv_full.reshape(model_width, 3 * local_width),
        preferred_element_type=jnp.float32,
    )
    projected = projected.reshape(group_size, 3, local_width)
    head_shape = (group_size, heads_local, head_size)
    query_heads = (
        (projected[:, 0] + bias_full[0].reshape(local_width))
        .astype(jnp.bfloat16)
        .reshape(head_shape)
    )
    key_heads = projected[:, 1].astype(jnp.bfloat16).reshape(head_shape)
    value_heads = (
        (projected[:, 2] + bias_full[1].reshape(local_width))
        .astype(jnp.bfloat16)
        .reshape(head_shape)
    )
    block_index = 0
    first_row = block_index * group_size
    scores = block_scores(query_heads, key_heads, first_row, slopes, lengths)
    row_max = jnp.max(scores, axis=-1, keepdims=True)
    exponent = jnp.exp(scores - row_max)
    row_sum = jnp.sum(exponent, axis=-1, keepdims=True)
    weights = (exponent / row_sum).astype(jnp.bfloat16)
    out_blocks = jnp.einsum(
        "hqk,khd->qhd", weights, value_heads, preferred_element_type=jnp.float32
    )
    lse_blocks = (row_max + jnp.log(row_sum))[..., 0]
    attended = out_blocks.reshape(group_size, local_width).astype(jnp.bfloat16)
    branch_attn = lax.psum_scatter(
        jnp.dot(attended, out_full, preferred_element_type=jnp.float32).astype(jnp.bfloat16),
        "tensor",
        scatter_dimension=0,
        tiled=True,
    ).astype(jnp.float32)
    middle = inputs + branch_attn + vec_full[2]
    normed_two = layer_norm(middle, vec_full[3], vec_full[4]).astype(jnp.bfloat16)
    group_two = lax.all_gather(normed_two, "tensor", axis=0, tiled=True)
    pre_act = jnp.dot(group_two, up_full, preferred_element_type=jnp.float32) + upbias_full.reshape(
        hidden_local
    )
    activated = gelu_tanh(pre_act).astype(jnp.bfloat16)
    branch_mlp = lax.psum_scatter(
        jnp.dot(activated, down_full, preferred_element_type=jnp.float32).astype(jnp.bfloat16),
        "tensor",
        scatter_dimension=0,
        tiled=True,
    ).astype(jnp.float32)
    output = (middle + branch_mlp + vec_full[5]).astype(jnp.bfloat16)
    qkv_back, out_back, up_back, down_back = (
        lax.all_gather(w_qkv, "dp", axis=0, tiled=True),
        lax.all_gather(w_out, "dp", axis=1, tiled=True),
        lax.all_gather(w_up, "dp", axis=0, tiled=True),
        lax.all_gather(w_down, "dp", axis=1, tiled=True),
    )
    grad_output = cotangent.astype(jnp.float32)
    grad_mlp = grad_output.astype(jnp.bfloat16)
    shard_rows = lax.all_gather(grad_mlp, "tensor", axis=0, tiled=True)
    used_rows = activated
    grad_weight = lax.dot_general(
        used_rows, shard_rows, (((0,), (0,)), ((), ())), preferred_element_type=jnp.float32
    )
    partial_value = lax.dot_general(
        shard_rows, down_back, (((1,), (1,)), ((), ())), preferred_element_type=jnp.float32
    )
    grad_down = grad_weight
    grad_act = partial_value
    _, gelu_back = jax.vjp(gelu_tanh, pre_act)
    grad_pre = gelu_back(grad_act)[0].astype(jnp.bfloat16)
    grad_upbias = jnp.sum(grad_pre.astype(jnp.float32), axis=0).reshape(upbias_full.shape)
    grad_up = lax.dot_general(
        group_two, grad_pre, (((0,), (0,)), ((), ())), preferred_element_type=jnp.float32
    )
    used_rows = grad_pre
    grad_normed_two = lax.psum_scatter(
        lax.dot_general(
            used_rows, up_back, (((1,), (1,)), ((), ())), preferred_element_type=jnp.float32
        ).astype(jnp.bfloat16),
        "tensor",
        scatter_dimension=0,
        tiled=True,
    ).astype(jnp.float32)
    _, norm_two_back = jax.vjp(layer_norm, middle, vec_full[3], vec_full[4])
    grad_mid_norm, grad_gain_two, grad_shift_two = norm_two_back(grad_normed_two)
    grad_middle = grad_output + grad_mid_norm
    grad_attn = grad_middle.astype(jnp.bfloat16)
    shard_rows = lax.all_gather(grad_attn, "tensor", axis=0, tiled=True)
    used_rows = attended
    grad_weight = lax.dot_general(
        used_rows, shard_rows, (((0,), (0,)), ((), ())), preferred_element_type=jnp.float32
    )
    partial_value = lax.dot_general(
        shard_rows, out_back, (((1,), (1,)), ((), ())), preferred_element_type=jnp.float32
    )
    grad_heads = partial_value.astype(jnp.bfloat16).reshape(head_shape)
    score_scale = head_size ** (-0.5)
    block_index = 0
    first_row = block_index * group_size
    scores = block_scores(query_heads, key_heads, first_row, slopes, lengths)
    probs = jnp.exp(scores - lse_blocks[:, first_row : first_row + group_size, None])
    weights = probs.astype(jnp.bfloat16)
    grad_probs = jnp.einsum(
        "qhd,khd->hqk", grad_heads, value_heads, preferred_element_type=jnp.float32
    )
    row_term = jnp.sum(probs * grad_probs, axis=-1, keepdims=True)
    grad_scores = (probs * (grad_probs - row_term)).astype(jnp.bfloat16)
    query_parts = (
        jnp.einsum("hqk,khd->qhd", grad_scores, key_heads, preferred_element_type=jnp.float32)
        * score_scale
    )
    grad_keys = (
        jnp.einsum("hqk,qhd->khd", grad_scores, query_heads, preferred_element_type=jnp.float32)
        * score_scale
    )
    grad_values = jnp.einsum(
        "hqk,qhd->khd", weights, grad_heads, preferred_element_type=jnp.float32
    )
    grad_query = query_parts.reshape(group_size, local_width).astype(jnp.bfloat16)
    grad_key = grad_keys.reshape(group_size, local_width).astype(jnp.bfloat16)
    grad_value = grad_values.reshape(group_size, local_width).astype(jnp.bfloat16)
    grad_proj = jnp.stack([grad_query, grad_key, grad_value], axis=1)
    grad_qvbias = jnp.stack(
        [
            jnp.sum(grad_query.astype(jnp.float32), axis=0),
            jnp.sum(grad_value.astype(jnp.float32), axis=0),
        ]
    ).reshape(bias_full.shape)
    grad_qkv = lax.dot_general(
        group_one, grad_proj, (((0,), (0,)), ((), ())), preferred_element_type=jnp.float32
    )
    used_rows = grad_proj
    grad_normed_one = lax.psum_scatter(
        lax.dot_general(
            used_rows, qkv_back, (((1, 2), (1, 2)), ((), ())), preferred_element_type=jnp.float32
        ).astype(jnp.bfloat16),
        "tensor",
        scatter_dimension=0,
        tiled=True,
    ).astype(jnp.float32)
    _, norm_one_back = jax.vjp(layer_norm, inputs, vec_full[0], vec_full[1])
    grad_in_norm, grad_gain_one, grad_shift_one = norm_one_back(grad_normed_one)
    grad_tokens = (grad_middle + grad_in_norm).astype(jnp.bfloat16)
    grad_vecs = jnp.stack(
        [
            grad_gain_one,
            grad_shift_one,
            jnp.sum(grad_middle, axis=0),
            grad_gain_two,
            grad_shift_two,
            jnp.sum(grad_output, axis=0),
        ]
    )
    sent_qkv, sent_qvbias, sent_out, sent_up, sent_upbias, sent_down, sent_vecs = (
        lax.psum_scatter(grad_qkv, "dp", scatter_dimension=0, tiled=True),
        lax.psum_scatter(grad_qvbias, "dp", scatter_dimension=2, tiled=True),
        lax.psum_scatter(grad_weight, "dp", scatter_dimension=1, tiled=True),
        lax.psum_scatter(grad_up, "dp", scatter_dimension=0, tiled=True),
        lax.psum_scatter(grad_upbias, "dp", scatter_dimension=1, tiled=True),
        lax.psum_scatter(grad_down, "dp", scatter_dimension=1, tiled=True),
        lax.psum_scatter(grad_vecs, "dp", scatter_dimension=1, tiled=True),
    )
    sent_vecs = lax.psum(sent_vecs, "tensor")
    return (
        output,
        grad_tokens,
        sent_vecs,
        sent_qkv,
        sent_qvbias,
        sent_out,
        sent_up,
        sent_upbias,
        sent_down,
    )


Z_COUNT, Y_COUNT, T_COUNT = 4, 2, 4
MESH_ID = pl.DeviceIdType.MESH
ANYWHERE = pl.BlockSpec(memory_space=pl.ANY)
IN_VMEM = pl.BlockSpec(memory_space=pltpu.VMEM)


class Place:
    def __init__(self):
        dp = lax.axis_index("dp")
        self.t = lax.axis_index("tensor")
        self.z = dp // Y_COUNT
        self.y = dp % Y_COUNT
        self.other_y = 1 - self.y
        self.dp = dp

    def owner(self, z_index, y_index):
        return z_index * Y_COUNT + y_index

    def z_next(self, step):
        return lax.rem(self.z + step, Z_COUNT)

    def z_prev(self, step):
        return lax.rem(self.z + Z_COUNT - step, Z_COUNT)

    def z_peer(self, step):
        return (self.owner(self.z_next(step), self.y), self.t)

    def y_peer(self):
        return (self.owner(self.z, self.other_y), self.t)

    def t_next(self, step):
        return lax.rem(self.t + step, T_COUNT)

    def t_peer(self, step):
        return (self.dp, self.t_next(step))

    def barrier(self):
        sem = pltpu.get_barrier_semaphore()
        peers = [self.z_peer(1), self.z_peer(Z_COUNT - 1)]
        peers += [self.y_peer()]
        peers += [self.t_peer(k) for k in range(1, T_COUNT)]
        for peer in peers:
            pl.semaphore_signal(sem, inc=1, device_id=peer, device_id_type=MESH_ID)
        pl.semaphore_wait(sem, len(peers))


def block_of(ref, owner, size, axis):
    start = pl.multiple_of(owner * size, size)
    if axis == 0:
        return ref.at[pl.ds(start, size), :]
    return ref.at[:, pl.ds(start, size)]


def remote(src, dst, send_sem, recv_sem, peer):
    return pltpu.make_async_remote_copy(
        src_ref=src,
        dst_ref=dst,
        send_sem=send_sem,
        recv_sem=recv_sem,
        device_id=peer,
        device_id_type=MESH_ID,
    )


class DpGather:
    def __init__(self, here, shard, full, axis, sems):
        self.here, self.shard, self.full, self.axis = here, shard, full, axis
        self.send, self.recv, self.own = sems
        self.size = shard.shape[axis]

    def slot(self, owner):
        return block_of(self.full, owner, self.size, self.axis)

    def fly(self, src, dst, index, peer):
        flight = remote(src, dst, self.send.at[index], self.recv.at[index], peer)
        flight.start()
        return flight

    def start(self):
        here = self.here
        mine = self.slot(here.dp)
        self.z_flights = [self.fly(self.shard, mine, 0, here.z_peer(1))]
        self.y_flights = [self.fly(self.shard, mine, 3, here.y_peer())]
        self.local = pltpu.make_async_copy(self.shard, mine, self.own)
        self.local.start()

    def step(self, k):
        here = self.here
        self.z_flights[k - 1].wait_recv()
        held = self.slot(here.owner(here.z_prev(k), here.y))
        if k < Z_COUNT - 1:
            self.z_flights.append(self.fly(held, held, k, here.z_peer(1)))
        self.y_flights.append(self.fly(held, held, 3 + k, here.y_peer()))

    def finish(self):
        for flight in self.y_flights:
            flight.wait_recv()
        for flight in self.z_flights + self.y_flights:
            flight.wait_send()
        self.local.wait()


class DpScatter:
    def __init__(self, here, part, total, axis, y_buf, z_out, z_in, sems):
        self.here, self.part, self.total, self.axis = here, part, total, axis
        self.y_buf, self.z_out, self.z_in = y_buf, z_out, z_in
        self.send, self.recv = sems
        self.size = total.shape[axis]
        self.y_flights, self.z_flights = [], []

    def slot(self, owner):
        return block_of(self.part, owner, self.size, self.axis)

    def fly(self, src, dst, index, peer):
        flight = remote(src, dst, self.send.at[index], self.recv.at[index], peer)
        flight.start()
        return flight

    def send_y(self, k):
        here = self.here
        src = self.slot(here.owner(here.z_prev(k), here.other_y))
        self.y_flights.append(self.fly(src, self.y_buf.at[k - 1], k - 1, here.y_peer()))

    def sum(self, k):
        here = self.here
        self.y_flights[k - 1].wait_recv()
        own = self.slot(here.owner(here.z_prev(k), here.y))[...].astype(jnp.float32)
        acc = own + self.y_buf[k - 1].astype(jnp.float32)
        if k > 1:
            self.z_flights[k - 2].wait_recv()
            acc = acc + self.z_in[k - 2].astype(jnp.float32)
        return acc

    def step(self, k):
        self.z_out[k - 1] = self.sum(k).astype(self.z_out.dtype)
        self.z_flights.append(
            self.fly(self.z_out.at[k - 1], self.z_in.at[k - 1], 3 + k, self.here.z_peer(1))
        )

    def finish(self):
        self.total[...] = self.sum(Z_COUNT)
        for flight in self.y_flights + self.z_flights:
            flight.wait_send()


class TensorGather:
    def __init__(self, here, full, rows, send, recv):
        self.here, self.full, self.rows = here, full, rows
        self.send, self.recv = send, recv

    def start(self, src=None):
        here = self.here
        mine = block_of(self.full, here.t, self.rows, 0)
        self.flights = []
        for k in (2, 3, 1):
            flight = remote(
                mine if src is None else src,
                mine,
                self.send.at[k - 1],
                self.recv.at[k - 1],
                here.t_peer(k),
            )
            flight.start()
            self.flights.append(flight)

    def finish(self):
        for flight in self.flights:
            flight.wait_recv()
        for flight in self.flights:
            flight.wait_send()


class TensorScatter:
    def __init__(self, here, part, buf, send, recv):
        self.here, self.part, self.buf = here, part, buf
        self.send, self.recv = send, recv
        self.rows = buf.shape[1]

    def start(self):
        here = self.here
        self.flights = []
        for k in (2, 3, 1):
            flight = remote(
                block_of(self.part, here.t_next(k), self.rows, 0),
                self.buf.at[k - 1],
                self.send.at[k - 1],
                self.recv.at[k - 1],
                here.t_peer(k),
            )
            flight.start()
            self.flights.append(flight)

    def total(self):
        for flight in self.flights:
            flight.wait_recv()
        acc = block_of(self.part, self.here.t, self.rows, 0)[...].astype(jnp.float32)
        for k in range(T_COUNT - 1):
            acc = acc + self.buf[k].astype(jnp.float32)
        return acc

    def finish(self):
        for flight in self.flights:
            flight.wait_send()


DMA = pltpu.SemaphoreType.DMA
gather_sems = [DMA((7,)), DMA((7,)), DMA]
pair_sems = [DMA((7,)), DMA((7,))]
tensor_sems = [DMA((3,)), DMA((3,))]


def scatter_scratch(block, dtype):
    return [
        pltpu.VMEM((4,) + block, dtype),
        pltpu.VMEM((3,) + block, dtype),
        pltpu.VMEM((3,) + block, dtype),
    ] + pair_sems


def call(kernel, name, outs, in_specs, out_specs, scratch, collective_id):
    return pl.pallas_call(
        kernel,
        name=name,
        out_shape=outs,
        in_specs=in_specs,
        out_specs=out_specs,
        scratch_shapes=scratch,
        compiler_params=pltpu.CompilerParams(
            collective_id=collective_id,
            has_side_effects=True,
            vmem_limit_bytes=44 * 1024 * 1024,
        ),
    )


def gather_kernel(
    tok, cot, small, qkv, out, up, tok_full, cot_full, small_full, qkv_full, out_full, up_full, *sems
):
    here = Place()
    here.barrier()
    rows = tok.shape[0]
    shards = (
        (small, small_full, 0),
        (qkv, qkv_full, 0),
        (out, out_full, 1),
        (up, up_full, 0),
    )
    gathers = [
        DpGather(here, shard, full, axis, sems[3 * i : 3 * i + 3])
        for i, (shard, full, axis) in enumerate(shards)
    ]
    rest = sems[3 * len(shards) :]
    across = []
    for i, (own, full) in enumerate(((tok, tok_full), (cot, cot_full))):
        local = pltpu.make_async_copy(own, block_of(full, here.t, rows, 0), rest[4 + i])
        local.start()
        moving = TensorGather(here, full, rows, rest[2 * i], rest[2 * i + 1])
        moving.start(own)
        across.append((local, moving))
    for item in gathers:
        item.start()
    for k in range(1, Z_COUNT):
        for item in gathers:
            item.step(k)
    for item in gathers:
        item.finish()
    for local, moving in across:
        moving.finish()
        local.wait()


def normalize(values):
    center = values - jnp.mean(values, axis=-1, keepdims=True)
    scale = lax.rsqrt(jnp.mean(center * center, axis=-1, keepdims=True) + epsilon)
    return center * scale, scale


def middle_kernel(
    part, tok, vec, down, mid, normed_full, down_full, buf, g_send, g_recv, g_own, s_send, s_recv, a_send, a_recv
):
    here = Place()
    here.barrier()
    scatter = TensorScatter(here, part, buf, s_send, s_recv)
    scatter.start()
    weights = DpGather(here, down, down_full, 1, (g_send, g_recv, g_own))
    weights.start()
    weights.step(1)
    rows = tok.shape[0]
    middle = tok[...].astype(jnp.float32) + scatter.total() + vec[2:3]
    mid[...] = middle
    hat, _ = normalize(middle)
    block_of(normed_full, here.t, rows, 0)[...] = (hat * vec[3:4] + vec[4:5]).astype(jnp.bfloat16)
    spread = TensorGather(here, normed_full, rows, a_send, a_recv)
    spread.start()
    weights.step(2)
    weights.step(3)
    spread.finish()
    weights.finish()
    scatter.finish()


def norm_back(grad, values, gain):
    hat, scale = normalize(values)
    e = grad * gain
    inner = scale * (
        e - jnp.mean(e, axis=-1, keepdims=True) - hat * jnp.mean(e * hat, axis=-1, keepdims=True)
    )
    gain_grad = jnp.sum(grad * hat, axis=0, keepdims=True)
    shift_grad = jnp.sum(grad, axis=0, keepdims=True)
    return inner, gain_grad, shift_grad


def back_kernel(
    part_norm, mid, cot, vec, grad_down, grad_mid, attn_full, sums, total_down,
    buf_norm, y_buf, z_out, z_in, d_send, d_recv, n_send, n_recv, a_send, a_recv
):
    here = Place()
    here.barrier()
    rows = mid.shape[0]
    first = TensorScatter(here, part_norm, buf_norm, n_send, n_recv)
    first.start()
    down = DpScatter(here, grad_down, total_down, 1, y_buf, z_out, z_in, (d_send, d_recv))
    down.send_y(1)
    down.send_y(2)
    down.step(1)
    down.send_y(3)
    down.send_y(4)
    grad_out = cot[...].astype(jnp.float32)
    inner, gain_grad, shift_grad = norm_back(first.total(), mid[...], vec[3:4])
    grad = grad_out + inner
    grad_mid[...] = grad
    block_of(attn_full, here.t, rows, 0)[...] = grad.astype(jnp.bfloat16)
    spread = TensorGather(here, attn_full, rows, a_send, a_recv)
    spread.start()
    down.step(2)
    zero = jnp.zeros_like(gain_grad)
    sums[0:1] = zero
    sums[1:2] = zero
    sums[2:3] = jnp.sum(grad, axis=0, keepdims=True)
    sums[3:4] = gain_grad
    sums[4:5] = shift_grad
    sums[5:6] = jnp.sum(grad_out, axis=0, keepdims=True)
    sums[6:7] = zero
    sums[7:8] = zero
    down.step(3)
    spread.finish()
    down.finish()
    first.finish()


def last_kernel(
    part, part_mlp, tok, mid, grad_mid, vec, sums, bias_rows, grad_out, grad_up, grad_qkv,
    grad_tok, result, total_small, total_out, total_up, total_qkv,
    buf, buf_mlp, small_part, small_mine, small_sum, small_buf,
    t_send, t_recv, m_send, m_recv, v_send, v_recv, *scratch
):
    here = Place()
    here.barrier()
    plan = ((grad_out, total_out, 1), (grad_up, total_up, 0), (grad_qkv, total_qkv, 0))
    big = []
    for i, (ref, total, axis) in enumerate(plan):
        group = scratch[5 * i : 5 * i + 5]
        item = DpScatter(here, ref, total, axis, *group[:3], group[3:])
        item.send_y(1)
        big.append(item)
    scatter = TensorScatter(here, part, buf, t_send, t_recv)
    scatter.start()
    second = TensorScatter(here, part_mlp, buf_mlp, m_send, m_recv)
    second.start()
    for item in big:
        item.send_y(2)
    for item in big:
        item.step(1)
        item.send_y(3)
    inner, gain_grad, shift_grad = norm_back(
        scatter.total(), tok[...].astype(jnp.float32), vec[0:1]
    )
    grad_tok[...] = (grad_mid[...] + inner).astype(jnp.bfloat16)
    width = total_small.shape[1]
    for d in range(Z_COUNT * Y_COUNT):
        cols = slice(d * width, (d + 1) * width)
        small_part[8 * d : 8 * d + 8] = sums[:, cols] + bias_rows[8 * d : 8 * d + 8]
        small_part[8 * d : 8 * d + 1] = gain_grad[:, cols]
        small_part[8 * d + 1 : 8 * d + 2] = shift_grad[:, cols]
    group = scratch[15:20]
    small = DpScatter(here, small_part, small_mine, 0, *group[:3], group[3:])
    for k in range(1, Z_COUNT + 1):
        small.send_y(k)
    for item in big:
        item.step(2)
        item.send_y(4)
    small.step(1)
    result[...] = (mid[...] + second.total() + vec[5:6]).astype(jnp.bfloat16)
    small.step(2)
    for item in big:
        item.step(3)
    small.step(3)
    small.finish()
    small_sum[...] = small_mine[...]
    flights = []
    for k in range(1, T_COUNT):
        flight = remote(
            small_sum, small_buf.at[k - 1], v_send.at[k - 1], v_recv.at[k - 1], here.t_peer(k)
        )
        flight.start()
        flights.append(flight)
    for item in big:
        item.finish()
    for flight in flights:
        flight.wait_recv()
    everyone = small_mine[...] + small_buf[0] + small_buf[1] + small_buf[2]
    row = lax.broadcasted_iota(jnp.int32, everyone.shape, 0)
    total_small[...] = jnp.where(row < 6, everyone, small_mine[...])
    for flight in flights:
        flight.wait_send()
    scatter.finish()
    second.finish()


def on_device_direct(
    tokens, cotangent, seg_lengths, vectors, w_qkv, qv_bias, w_out, w_up, up_bias, w_down
):
    bf16, f32 = jnp.bfloat16, jnp.float32
    rows, width = tokens.shape
    heads, head_part = qv_bias.shape[1], qv_bias.shape[2]
    dp, cols = Z_COUNT * Y_COUNT, vectors.shape[1]
    head_size = head_part * dp
    group_size = rows * T_COUNT
    local_width = w_qkv.shape[2]
    hidden = w_up.shape[1]
    up_part = up_bias.shape[1]
    lengths = seg_lengths[0]
    shape = jax.ShapeDtypeStruct
    qkv_wide = 3 * local_width
    qv_row = jnp.pad(qv_bias.reshape(1, -1), ((0, 0), (0, cols - qv_bias.size)))
    small = jnp.concatenate(
        [vectors, qv_row, up_bias.reshape(1, cols), jnp.zeros((8, cols), f32)]
    ).astype(bf16)
    tok_full, cot_full, small_full, qkv_full, out_full, up_full = call(
        gather_kernel,
        "gather_inputs",
        [
            shape((group_size, width), bf16),
            shape((group_size, width), bf16),
            shape((dp * 16, cols), bf16),
            shape((width, qkv_wide), bf16),
            shape((local_width, width), bf16),
            shape((width, hidden), bf16),
        ],
        [ANYWHERE] * 6,
        [ANYWHERE] * 6,
        gather_sems * 4 + tensor_sems * 2 + [DMA, DMA],
        1,
    )(tokens, cotangent, small, w_qkv.reshape(-1, qkv_wide), w_out, w_up)
    small_full = small_full.reshape(dp, 16, cols).astype(f32)
    vec_full = small_full[:, :8].transpose(1, 0, 2).reshape(8, width)
    bias_full = (
        small_full[:, 6, : qv_bias.size]
        .reshape(dp, 2, heads, head_part)
        .transpose(1, 2, 0, 3)
        .reshape(2, local_width)
    )
    upbias_full = small_full[:, 7].reshape(dp, heads, up_part).transpose(1, 0, 2).reshape(hidden)

    head_ids = lax.axis_index("tensor") * heads + jnp.arange(heads, dtype=jnp.int32)
    slopes = jnp.exp2(-8.0 * (head_ids + 1).astype(f32) / (heads * T_COUNT))
    group_one = layer_norm(tok_full.astype(f32), vec_full[0], vec_full[1]).astype(bf16)
    projected = jnp.dot(group_one, qkv_full, preferred_element_type=f32)
    projected = projected.reshape(group_size, 3, local_width)
    head_shape = (group_size, heads, head_size)
    query_heads = (projected[:, 0] + bias_full[0]).astype(bf16).reshape(head_shape)
    key_heads = projected[:, 1].astype(bf16).reshape(head_shape)
    value_heads = (projected[:, 2] + bias_full[1]).astype(bf16).reshape(head_shape)
    scores = block_scores(query_heads, key_heads, 0, slopes, lengths)
    row_max = jnp.max(scores, axis=-1, keepdims=True)
    exponent = jnp.exp(scores - row_max)
    row_sum = jnp.sum(exponent, axis=-1, keepdims=True)
    probs = exponent / row_sum
    weights = probs.astype(bf16)
    attended = (
        jnp.einsum("hqk,khd->qhd", weights, value_heads, preferred_element_type=f32)
        .reshape(group_size, local_width)
        .astype(bf16)
    )
    part_attn = jnp.dot(attended, out_full, preferred_element_type=f32).astype(bf16)

    middle, group_two, down_full = call(
        middle_kernel,
        "middle",
        [
            shape((rows, width), f32),
            shape((group_size, width), bf16),
            shape((hidden, width), bf16),
        ],
        [IN_VMEM, IN_VMEM, IN_VMEM, ANYWHERE],
        [IN_VMEM, IN_VMEM, ANYWHERE],
        [pltpu.VMEM((3, rows, width), bf16)] + gather_sems + tensor_sems * 2,
        2,
    )(part_attn, tokens, vec_full, w_down)

    contract_rows = (((0,), (0,)), ((), ()))
    contract_cols = (((1,), (1,)), ((), ()))
    pre_act = jnp.dot(group_two, up_full, preferred_element_type=f32) + upbias_full
    activated, gelu_back = jax.vjp(gelu_tanh, pre_act)
    activated = activated.astype(bf16)
    part_mlp = jnp.dot(activated, down_full, preferred_element_type=f32).astype(bf16)
    grad_act = lax.dot_general(cot_full, down_full, contract_cols, preferred_element_type=f32)
    grad_pre = gelu_back(grad_act)[0].astype(bf16)
    part_norm = lax.dot_general(
        grad_pre, up_full, contract_cols, preferred_element_type=f32
    ).astype(bf16)
    grad_down = lax.dot_general(
        activated, cot_full, contract_rows, preferred_element_type=f32
    ).astype(bf16)
    grad_up = lax.dot_general(
        group_two, grad_pre, contract_rows, preferred_element_type=f32
    ).astype(bf16)
    grad_upbias = jnp.sum(grad_pre.astype(f32), axis=0)

    grad_middle, attn_full, sums, total_down = call(
        back_kernel,
        "back",
        [
            shape((rows, width), f32),
            shape((group_size, width), bf16),
            shape((8, width), f32),
            shape((hidden, cols), f32),
        ],
        [IN_VMEM] * 5,
        [IN_VMEM] * 4,
        [pltpu.VMEM((3, rows, width), bf16)]
        + scatter_scratch((hidden, cols), bf16)
        + tensor_sems * 2,
        3,
    )(part_norm, middle, cotangent, vec_full, grad_down)

    grad_out = lax.dot_general(
        attended, attn_full, contract_rows, preferred_element_type=f32
    ).astype(bf16)
    grad_heads = (
        lax.dot_general(attn_full, out_full, contract_cols, preferred_element_type=f32)
        .astype(bf16)
        .reshape(head_shape)
    )
    score_scale = head_size ** (-0.5)
    grad_probs = jnp.einsum("qhd,khd->hqk", grad_heads, value_heads, preferred_element_type=f32)
    row_term = jnp.sum(probs * grad_probs, axis=-1, keepdims=True)
    grad_scores = (probs * (grad_probs - row_term)).astype(bf16)
    grad_query = (
        jnp.einsum("hqk,khd->qhd", grad_scores, key_heads, preferred_element_type=f32) * score_scale
    )
    grad_keys = (
        jnp.einsum("hqk,qhd->khd", grad_scores, query_heads, preferred_element_type=f32)
        * score_scale
    )
    grad_values = jnp.einsum("hqk,qhd->khd", weights, grad_heads, preferred_element_type=f32)
    grad_proj = jnp.concatenate(
        [item.reshape(group_size, local_width).astype(bf16) for item in (grad_query, grad_keys, grad_values)],
        axis=1,
    )
    bias_sums = jnp.sum(grad_proj.astype(f32), axis=0)
    grad_qvbias = jnp.stack([bias_sums[:local_width], bias_sums[2 * local_width :]])
    grad_qkv = lax.dot_general(
        group_one, grad_proj, contract_rows, preferred_element_type=f32
    ).astype(bf16)
    part_first = lax.dot_general(
        grad_proj, qkv_full, contract_cols, preferred_element_type=f32
    ).astype(bf16)
    qv_rows = (
        grad_qvbias.reshape(2, heads, dp, head_part).transpose(2, 0, 1, 3).reshape(dp, 1, qv_bias.size)
    )
    qv_rows = jnp.pad(qv_rows, ((0, 0), (0, 0), (0, cols - qv_bias.size)))
    up_rows = grad_upbias.reshape(heads, dp, up_part).transpose(1, 0, 2).reshape(dp, 1, cols)
    bias_rows = jnp.concatenate([jnp.zeros((dp, 6, cols), f32), qv_rows, up_rows], axis=1)
    bias_rows = bias_rows.reshape(dp * 8, cols)

    grad_tokens, output, total_small, total_out, total_up, total_qkv = call(
        last_kernel,
        "last",
        [
            shape((rows, width), bf16),
            shape((rows, width), bf16),
            shape((8, cols), f32),
            shape((local_width, cols), f32),
            shape((width // dp, hidden), f32),
            shape((width // dp, qkv_wide), f32),
        ],
        [IN_VMEM] * 11,
        [IN_VMEM] * 6,
        [
            pltpu.VMEM((3, rows, width), bf16),
            pltpu.VMEM((3, rows, width), bf16),
            pltpu.VMEM((8 * dp, cols), f32),
            pltpu.VMEM((8, cols), f32),
            pltpu.VMEM((8, cols), f32),
            pltpu.VMEM((3, 8, cols), f32),
        ]
        + tensor_sems * 3
        + scatter_scratch((local_width, cols), bf16)
        + scatter_scratch((width // dp, hidden), bf16)
        + scatter_scratch((width // dp, qkv_wide), bf16)
        + scatter_scratch((8, cols), f32),
        4,
    )(part_first, part_mlp, tokens, middle, grad_middle, vec_full, sums, bias_rows, grad_out, grad_up, grad_qkv)
    return (
        output,
        grad_tokens,
        total_small[:6],
        total_qkv.reshape(w_qkv.shape),
        total_small[6, : qv_bias.size].reshape(qv_bias.shape),
        total_out,
        total_up,
        total_small[7].reshape(up_bias.shape),
        total_down,
    )


def solution(mesh):
    direct = mesh.shape["dp"] == Z_COUNT * Y_COUNT and mesh.shape["tensor"] == T_COUNT
    return jax.shard_map(
        on_device_direct if direct else on_device,
        mesh=mesh,
        in_specs=(
            P(("dp", "tensor"), None),
            P(("dp", "tensor"), None),
            P("dp", None),
            P(None, "dp"),
            P("dp", None, "tensor"),
            P(None, "tensor", "dp"),
            P("tensor", "dp"),
            P("dp", "tensor"),
            P("tensor", "dp"),
            P("tensor", "dp"),
        ),
        out_specs=(
            P(("dp", "tensor"), None),
            P(("dp", "tensor"), None),
            P(None, "dp"),
            P("dp", None, "tensor"),
            P(None, "tensor", "dp"),
            P("tensor", "dp"),
            P("dp", "tensor"),
            P("tensor", "dp"),
            P("tensor", "dp"),
        ),
        check_vma=False,
    )
```

```python
import jax
import jax.numpy as jnp
from jax import lax
from jax.experimental import pallas as pl
from jax.experimental.pallas import tpu as pltpu
from jax.sharding import PartitionSpec as P

epsilon = 1e-05
masked_score = -1e30


def layer_norm(values, gain_vec, shift_vec):
    center = values - jnp.mean(values, axis=-1, keepdims=True)
    spread = jnp.mean(center * center, axis=-1, keepdims=True)
    return center * lax.rsqrt(spread + epsilon) * gain_vec + shift_vec


def gelu_tanh(values):
    return jax.nn.gelu(values, approximate=True)


def doc_number(positions, lengths):
    doc_ends = jnp.cumsum(lengths)
    return jnp.sum((positions[:, None] >= doc_ends[None, :]).astype(jnp.int32), axis=1)


def block_scores(query_block, key_heads, first_row, slopes, lengths):
    block_size = query_block.shape[0]
    group_size = key_heads.shape[0]
    score_scale = query_block.shape[-1] ** (-0.5)
    scores = (
        jnp.einsum("qhd,khd->hqk", query_block, key_heads, preferred_element_type=jnp.float32)
        * score_scale
    )
    query_pos = first_row + jnp.arange(block_size, dtype=jnp.int32)
    key_pos = jnp.arange(group_size, dtype=jnp.int32)
    offset = (query_pos[:, None] - key_pos[None, :]).astype(jnp.float32)
    scores = scores - slopes[:, None, None] * offset[None]
    same_doc = doc_number(query_pos, lengths)[:, None] == doc_number(key_pos, lengths)[None, :]
    allowed = same_doc & (key_pos[None, :] <= query_pos[:, None])
    return jnp.where(allowed[None], scores, masked_score)


def on_device(
    tokens, cotangent, seg_lengths, vectors, w_qkv, qv_bias, w_out, w_up, up_bias, w_down
):
    model_width = tokens.shape[1]
    tensor_count = lax.axis_size("tensor")
    lengths = seg_lengths[0]
    gathered = (
        lax.all_gather(w_qkv, "dp", axis=0, tiled=True),
        lax.all_gather(qv_bias.astype(jnp.bfloat16), "dp", axis=2, tiled=True).astype(
            qv_bias.dtype
        ),
        lax.all_gather(w_out, "dp", axis=1, tiled=True),
        lax.all_gather(w_up, "dp", axis=0, tiled=True),
        lax.all_gather(up_bias.astype(jnp.bfloat16), "dp", axis=1, tiled=True).astype(
            up_bias.dtype
        ),
        lax.all_gather(w_down, "dp", axis=1, tiled=True),
        lax.all_gather(vectors.astype(jnp.bfloat16), "dp", axis=1, tiled=True).astype(
            vectors.dtype
        ),
    )
    qkv_full, bias_full, out_full, up_full, upbias_full, down_full, vec_full = gathered
    local_width = qkv_full.shape[2]
    heads_local = bias_full.shape[1]
    head_size = bias_full.shape[2]
    hidden_local = up_full.shape[1]
    head_ids = lax.axis_index("tensor") * heads_local + jnp.arange(heads_local, dtype=jnp.int32)
    slopes = jnp.exp2(-8.0 * (head_ids + 1).astype(jnp.float32) / (heads_local * tensor_count))
    inputs = tokens.astype(jnp.float32)
    normed_one = layer_norm(inputs, vec_full[0], vec_full[1]).astype(jnp.bfloat16)
    group_one = lax.all_gather(normed_one, "tensor", axis=0, tiled=True)
    group_size = group_one.shape[0]
    projected = jnp.dot(
        group_one,
        qkv_full.reshape(model_width, 3 * local_width),
        preferred_element_type=jnp.float32,
    )
    projected = projected.reshape(group_size, 3, local_width)
    head_shape = (group_size, heads_local, head_size)
    query_heads = (
        (projected[:, 0] + bias_full[0].reshape(local_width))
        .astype(jnp.bfloat16)
        .reshape(head_shape)
    )
    key_heads = projected[:, 1].astype(jnp.bfloat16).reshape(head_shape)
    value_heads = (
        (projected[:, 2] + bias_full[1].reshape(local_width))
        .astype(jnp.bfloat16)
        .reshape(head_shape)
    )
    block_index = 0
    first_row = block_index * group_size
    scores = block_scores(query_heads, key_heads, first_row, slopes, lengths)
    row_max = jnp.max(scores, axis=-1, keepdims=True)
    exponent = jnp.exp(scores - row_max)
    row_sum = jnp.sum(exponent, axis=-1, keepdims=True)
    weights = (exponent / row_sum).astype(jnp.bfloat16)
    out_blocks = jnp.einsum(
        "hqk,khd->qhd", weights, value_heads, preferred_element_type=jnp.float32
    )
    lse_blocks = (row_max + jnp.log(row_sum))[..., 0]
    attended = out_blocks.reshape(group_size, local_width).astype(jnp.bfloat16)
    branch_attn = lax.psum_scatter(
        jnp.dot(attended, out_full, preferred_element_type=jnp.float32).astype(jnp.bfloat16),
        "tensor",
        scatter_dimension=0,
        tiled=True,
    ).astype(jnp.float32)
    middle = inputs + branch_attn + vec_full[2]
    normed_two = layer_norm(middle, vec_full[3], vec_full[4]).astype(jnp.bfloat16)
    group_two = lax.all_gather(normed_two, "tensor", axis=0, tiled=True)
    pre_act = jnp.dot(group_two, up_full, preferred_element_type=jnp.float32) + upbias_full.reshape(
        hidden_local
    )
    activated = gelu_tanh(pre_act).astype(jnp.bfloat16)
    branch_mlp = lax.psum_scatter(
        jnp.dot(activated, down_full, preferred_element_type=jnp.float32).astype(jnp.bfloat16),
        "tensor",
        scatter_dimension=0,
        tiled=True,
    ).astype(jnp.float32)
    output = (middle + branch_mlp + vec_full[5]).astype(jnp.bfloat16)
    qkv_back, out_back, up_back, down_back = (
        lax.all_gather(w_qkv, "dp", axis=0, tiled=True),
        lax.all_gather(w_out, "dp", axis=1, tiled=True),
        lax.all_gather(w_up, "dp", axis=0, tiled=True),
        lax.all_gather(w_down, "dp", axis=1, tiled=True),
    )
    grad_output = cotangent.astype(jnp.float32)
    grad_mlp = grad_output.astype(jnp.bfloat16)
    shard_rows = lax.all_gather(grad_mlp, "tensor", axis=0, tiled=True)
    used_rows = activated
    grad_weight = lax.dot_general(
        used_rows, shard_rows, (((0,), (0,)), ((), ())), preferred_element_type=jnp.float32
    )
    partial_value = lax.dot_general(
        shard_rows, down_back, (((1,), (1,)), ((), ())), preferred_element_type=jnp.float32
    )
    grad_down = grad_weight
    grad_act = partial_value
    _, gelu_back = jax.vjp(gelu_tanh, pre_act)
    grad_pre = gelu_back(grad_act)[0].astype(jnp.bfloat16)
    grad_upbias = jnp.sum(grad_pre.astype(jnp.float32), axis=0).reshape(upbias_full.shape)
    grad_up = lax.dot_general(
        group_two, grad_pre, (((0,), (0,)), ((), ())), preferred_element_type=jnp.float32
    )
    used_rows = grad_pre
    grad_normed_two = lax.psum_scatter(
        lax.dot_general(
            used_rows, up_back, (((1,), (1,)), ((), ())), preferred_element_type=jnp.float32
        ).astype(jnp.bfloat16),
        "tensor",
        scatter_dimension=0,
        tiled=True,
    ).astype(jnp.float32)
    _, norm_two_back = jax.vjp(layer_norm, middle, vec_full[3], vec_full[4])
    grad_mid_norm, grad_gain_two, grad_shift_two = norm_two_back(grad_normed_two)
    grad_middle = grad_output + grad_mid_norm
    grad_attn = grad_middle.astype(jnp.bfloat16)
    shard_rows = lax.all_gather(grad_attn, "tensor", axis=0, tiled=True)
    used_rows = attended
    grad_weight = lax.dot_general(
        used_rows, shard_rows, (((0,), (0,)), ((), ())), preferred_element_type=jnp.float32
    )
    partial_value = lax.dot_general(
        shard_rows, out_back, (((1,), (1,)), ((), ())), preferred_element_type=jnp.float32
    )
    grad_heads = partial_value.astype(jnp.bfloat16).reshape(head_shape)
    score_scale = head_size ** (-0.5)
    block_index = 0
    first_row = block_index * group_size
    scores = block_scores(query_heads, key_heads, first_row, slopes, lengths)
    probs = jnp.exp(scores - lse_blocks[:, first_row : first_row + group_size, None])
    weights = probs.astype(jnp.bfloat16)
    grad_probs = jnp.einsum(
        "qhd,khd->hqk", grad_heads, value_heads, preferred_element_type=jnp.float32
    )
    row_term = jnp.sum(probs * grad_probs, axis=-1, keepdims=True)
    grad_scores = (probs * (grad_probs - row_term)).astype(jnp.bfloat16)
    query_parts = (
        jnp.einsum("hqk,khd->qhd", grad_scores, key_heads, preferred_element_type=jnp.float32)
        * score_scale
    )
    grad_keys = (
        jnp.einsum("hqk,qhd->khd", grad_scores, query_heads, preferred_element_type=jnp.float32)
        * score_scale
    )
    grad_values = jnp.einsum(
        "hqk,qhd->khd", weights, grad_heads, preferred_element_type=jnp.float32
    )
    grad_query = query_parts.reshape(group_size, local_width).astype(jnp.bfloat16)
    grad_key = grad_keys.reshape(group_size, local_width).astype(jnp.bfloat16)
    grad_value = grad_values.reshape(group_size, local_width).astype(jnp.bfloat16)
    grad_proj = jnp.stack([grad_query, grad_key, grad_value], axis=1)
    grad_qvbias = jnp.stack(
        [
            jnp.sum(grad_query.astype(jnp.float32), axis=0),
            jnp.sum(grad_value.astype(jnp.float32), axis=0),
        ]
    ).reshape(bias_full.shape)
    grad_qkv = lax.dot_general(
        group_one, grad_proj, (((0,), (0,)), ((), ())), preferred_element_type=jnp.float32
    )
    used_rows = grad_proj
    grad_normed_one = lax.psum_scatter(
        lax.dot_general(
            used_rows, qkv_back, (((1, 2), (1, 2)), ((), ())), preferred_element_type=jnp.float32
        ).astype(jnp.bfloat16),
        "tensor",
        scatter_dimension=0,
        tiled=True,
    ).astype(jnp.float32)
    _, norm_one_back = jax.vjp(layer_norm, inputs, vec_full[0], vec_full[1])
    grad_in_norm, grad_gain_one, grad_shift_one = norm_one_back(grad_normed_one)
    grad_tokens = (grad_middle + grad_in_norm).astype(jnp.bfloat16)
    grad_vecs = jnp.stack(
        [
            grad_gain_one,
            grad_shift_one,
            jnp.sum(grad_middle, axis=0),
            grad_gain_two,
            grad_shift_two,
            jnp.sum(grad_output, axis=0),
        ]
    )
    sent_qkv, sent_qvbias, sent_out, sent_up, sent_upbias, sent_down, sent_vecs = (
        lax.psum_scatter(grad_qkv, "dp", scatter_dimension=0, tiled=True),
        lax.psum_scatter(grad_qvbias, "dp", scatter_dimension=2, tiled=True),
        lax.psum_scatter(grad_weight, "dp", scatter_dimension=1, tiled=True),
        lax.psum_scatter(grad_up, "dp", scatter_dimension=0, tiled=True),
        lax.psum_scatter(grad_upbias, "dp", scatter_dimension=1, tiled=True),
        lax.psum_scatter(grad_down, "dp", scatter_dimension=1, tiled=True),
        lax.psum_scatter(grad_vecs, "dp", scatter_dimension=1, tiled=True),
    )
    sent_vecs = lax.psum(sent_vecs, "tensor")
    return (
        output,
        grad_tokens,
        sent_vecs,
        sent_qkv,
        sent_qvbias,
        sent_out,
        sent_up,
        sent_upbias,
        sent_down,
    )


Z_COUNT, Y_COUNT, T_COUNT = 4, 2, 4
MESH_ID = pl.DeviceIdType.MESH
ANYWHERE = pl.BlockSpec(memory_space=pl.ANY)
IN_VMEM = pl.BlockSpec(memory_space=pltpu.VMEM)


class Place:
    def __init__(self):
        dp = lax.axis_index("dp")
        self.t = lax.axis_index("tensor")
        self.z = dp // Y_COUNT
        self.y = dp % Y_COUNT
        self.other_y = 1 - self.y
        self.dp = dp

    def owner(self, z_index, y_index):
        return z_index * Y_COUNT + y_index

    def z_next(self, step):
        return lax.rem(self.z + step, Z_COUNT)

    def z_prev(self, step):
        return lax.rem(self.z + Z_COUNT - step, Z_COUNT)

    def z_peer(self, step):
        return (self.owner(self.z_next(step), self.y), self.t)

    def y_peer(self):
        return (self.owner(self.z, self.other_y), self.t)

    def t_next(self, step):
        return lax.rem(self.t + step, T_COUNT)

    def t_peer(self, step):
        return (self.dp, self.t_next(step))

    def barrier(self):
        sem = pltpu.get_barrier_semaphore()
        peers = [self.z_peer(1), self.z_peer(Z_COUNT - 1)]
        peers += [self.y_peer()]
        peers += [self.t_peer(k) for k in range(1, T_COUNT)]
        for peer in peers:
            pl.semaphore_signal(sem, inc=1, device_id=peer, device_id_type=MESH_ID)
        pl.semaphore_wait(sem, len(peers))


def block_of(ref, owner, size, axis):
    start = pl.multiple_of(owner * size, size)
    if axis == 0:
        return ref.at[pl.ds(start, size), :]
    return ref.at[:, pl.ds(start, size)]


def remote(src, dst, send_sem, recv_sem, peer):
    return pltpu.make_async_remote_copy(
        src_ref=src,
        dst_ref=dst,
        send_sem=send_sem,
        recv_sem=recv_sem,
        device_id=peer,
        device_id_type=MESH_ID,
    )


class DpGather:
    def __init__(self, here, shard, full, axis, sems):
        self.here, self.shard, self.full, self.axis = here, shard, full, axis
        self.send, self.recv, self.own = sems
        self.size = shard.shape[axis]

    def slot(self, owner):
        return block_of(self.full, owner, self.size, self.axis)

    def fly(self, src, dst, index, peer):
        flight = remote(src, dst, self.send.at[index], self.recv.at[index], peer)
        flight.start()
        return flight

    def start(self):
        here = self.here
        mine = self.slot(here.dp)
        self.z_flights = [self.fly(self.shard, mine, 0, here.z_peer(1))]
        self.y_flights = [self.fly(self.shard, mine, 3, here.y_peer())]
        self.local = pltpu.make_async_copy(self.shard, mine, self.own)
        self.local.start()

    def step(self, k):
        here = self.here
        self.z_flights[k - 1].wait_recv()
        held = self.slot(here.owner(here.z_prev(k), here.y))
        if k < Z_COUNT - 1:
            self.z_flights.append(self.fly(held, held, k, here.z_peer(1)))
        self.y_flights.append(self.fly(held, held, 3 + k, here.y_peer()))

    def finish(self):
        for flight in self.y_flights:
            flight.wait_recv()
        for flight in self.z_flights + self.y_flights:
            flight.wait_send()
        self.local.wait()


class DpScatter:
    def __init__(self, here, part, total, axis, y_buf, z_out, z_in, sems, own=None):
        self.own, self.locals = own, []
        self.here, self.part, self.total, self.axis = here, part, total, axis
        self.y_buf, self.z_out, self.z_in = y_buf, z_out, z_in
        self.send, self.recv = sems
        self.size = y_buf.shape[1 + axis]
        self.y_flights, self.z_flights = [], []

    def slot(self, owner):
        return block_of(self.part, owner, self.size, self.axis)

    def fly(self, src, dst, index, peer):
        flight = remote(src, dst, self.send.at[index], self.recv.at[index], peer)
        flight.start()
        return flight

    def send_y(self, k):
        here = self.here
        src = self.slot(here.owner(here.z_prev(k), here.other_y))
        self.y_flights.append(self.fly(src, self.y_buf.at[k - 1], k - 1, here.y_peer()))
        if self.own is not None:
            mine = self.slot(here.owner(here.z_prev(k), here.y))
            local = pltpu.make_async_copy(mine, self.own[0].at[k - 1], self.own[1].at[k - 1])
            local.start()
            self.locals.append(local)

    def sum(self, k):
        here = self.here
        self.y_flights[k - 1].wait_recv()
        if self.own is None:
            own = self.slot(here.owner(here.z_prev(k), here.y))[...]
        else:
            self.locals[k - 1].wait()
            own = self.own[0][k - 1]
        acc = own.astype(jnp.float32) + self.y_buf[k - 1].astype(jnp.float32)
        if k > 1:
            self.z_flights[k - 2].wait_recv()
            acc = acc + self.z_in[k - 2].astype(jnp.float32)
        return acc

    def step(self, k):
        self.z_out[k - 1] = self.sum(k).astype(self.z_out.dtype)
        self.z_flights.append(
            self.fly(self.z_out.at[k - 1], self.z_in.at[k - 1], 3 + k, self.here.z_peer(1))
        )

    def finish(self):
        acc = self.sum(Z_COUNT)
        if len(self.total.shape) == 3:
            width = self.total.shape[2]
            for i in range(self.total.shape[0]):
                self.total[i] = acc[:, i * width : (i + 1) * width]
        else:
            self.total[...] = acc
        for flight in self.y_flights + self.z_flights:
            flight.wait_send()


class TensorGather:
    def __init__(self, here, full, rows, send, recv):
        self.here, self.full, self.rows = here, full, rows
        self.send, self.recv = send, recv

    def start(self, src=None):
        here = self.here
        mine = block_of(self.full, here.t, self.rows, 0)
        self.flights = []
        for k in (2, 3, 1):
            flight = remote(
                mine if src is None else src,
                mine,
                self.send.at[k - 1],
                self.recv.at[k - 1],
                here.t_peer(k),
            )
            flight.start()
            self.flights.append(flight)

    def finish(self):
        for flight in self.flights:
            flight.wait_recv()
        for flight in self.flights:
            flight.wait_send()


class TensorScatter:
    def __init__(self, here, part, buf, send, recv, own=None):
        self.own = own
        self.here, self.part, self.buf = here, part, buf
        self.send, self.recv = send, recv
        self.rows = buf.shape[1]

    def start(self):
        here = self.here
        self.flights = []
        for k in (2, 3, 1):
            flight = remote(
                block_of(self.part, here.t_next(k), self.rows, 0),
                self.buf.at[k - 1],
                self.send.at[k - 1],
                self.recv.at[k - 1],
                here.t_peer(k),
            )
            flight.start()
            self.flights.append(flight)
        if self.own is not None:
            mine = block_of(self.part, here.t, self.rows, 0)
            self.local = pltpu.make_async_copy(mine, self.own[0], self.own[1])
            self.local.start()

    def total(self):
        for flight in self.flights:
            flight.wait_recv()
        if self.own is None:
            acc = block_of(self.part, self.here.t, self.rows, 0)[...].astype(jnp.float32)
        else:
            self.local.wait()
            acc = self.own[0][...].astype(jnp.float32)
        for k in range(T_COUNT - 1):
            acc = acc + self.buf[k].astype(jnp.float32)
        return acc

    def finish(self):
        for flight in self.flights:
            flight.wait_send()


DMA = pltpu.SemaphoreType.DMA
gather_sems = [DMA((7,)), DMA((7,)), DMA]
pair_sems = [DMA((7,)), DMA((7,))]
tensor_sems = [DMA((3,)), DMA((3,))]


def scatter_scratch(block, dtype):
    return [
        pltpu.VMEM((4,) + block, dtype),
        pltpu.VMEM((3,) + block, dtype),
        pltpu.VMEM((3,) + block, dtype),
    ] + pair_sems


def call(kernel, name, outs, in_specs, out_specs, scratch, collective_id):
    return pl.pallas_call(
        kernel,
        name=name,
        out_shape=outs,
        in_specs=in_specs,
        out_specs=out_specs,
        scratch_shapes=scratch,
        compiler_params=pltpu.CompilerParams(
            collective_id=collective_id,
            has_side_effects=True,
            vmem_limit_bytes=(56 if collective_id == 4 else 24) * 1024 * 1024,
        ),
    )


def gather_kernel(
    tok, cot, small, qkv, out, up, tok_full, cot_full, small_full, qkv_full, out_full, up_full, *sems
):
    here = Place()
    here.barrier()
    rows = tok.shape[0]
    shards = (
        (small, small_full, 0),
        (qkv, qkv_full, 0),
        (out, out_full, 1),
        (up, up_full, 0),
    )
    gathers = [
        DpGather(here, shard, full, axis, sems[3 * i : 3 * i + 3])
        for i, (shard, full, axis) in enumerate(shards)
    ]
    rest = sems[3 * len(shards) :]
    across = []
    for i, (own, full) in enumerate(((tok, tok_full), (cot, cot_full))):
        local = pltpu.make_async_copy(own, block_of(full, here.t, rows, 0), rest[4 + i])
        local.start()
        moving = TensorGather(here, full, rows, rest[2 * i], rest[2 * i + 1])
        moving.start(own)
        across.append((local, moving))
    for item in gathers:
        item.start()
    for k in range(1, Z_COUNT):
        for item in gathers:
            item.step(k)
    for item in gathers:
        item.finish()
    for local, moving in across:
        moving.finish()
        local.wait()


def normalize(values):
    center = values - jnp.mean(values, axis=-1, keepdims=True)
    scale = lax.rsqrt(jnp.mean(center * center, axis=-1, keepdims=True) + epsilon)
    return center * scale, scale


def middle_kernel(
    part, tok, vec, down, mid, normed_full, down_full, buf, g_send, g_recv, g_own, s_send, s_recv, a_send, a_recv
):
    here = Place()
    here.barrier()
    scatter = TensorScatter(here, part, buf, s_send, s_recv)
    scatter.start()
    weights = DpGather(here, down, down_full, 1, (g_send, g_recv, g_own))
    weights.start()
    weights.step(1)
    rows = tok.shape[0]
    middle = tok[...].astype(jnp.float32) + scatter.total() + vec[2:3]
    mid[...] = middle
    hat, _ = normalize(middle)
    block_of(normed_full, here.t, rows, 0)[...] = (hat * vec[3:4] + vec[4:5]).astype(jnp.bfloat16)
    spread = TensorGather(here, normed_full, rows, a_send, a_recv)
    spread.start()
    weights.step(2)
    weights.step(3)
    spread.finish()
    weights.finish()
    scatter.finish()


def norm_back(grad, values, gain):
    hat, scale = normalize(values)
    e = grad * gain
    inner = scale * (
        e - jnp.mean(e, axis=-1, keepdims=True) - hat * jnp.mean(e * hat, axis=-1, keepdims=True)
    )
    gain_grad = jnp.sum(grad * hat, axis=0, keepdims=True)
    shift_grad = jnp.sum(grad, axis=0, keepdims=True)
    return inner, gain_grad, shift_grad


def back_kernel(
    part_norm, mid, cot, vec, grad_down, grad_mid, attn_full, sums, total_down,
    buf_norm, y_buf, z_out, z_in, d_send, d_recv, n_send, n_recv, a_send, a_recv
):
    here = Place()
    here.barrier()
    rows = mid.shape[0]
    first = TensorScatter(here, part_norm, buf_norm, n_send, n_recv)
    first.start()
    down = DpScatter(here, grad_down, total_down, 1, y_buf, z_out, z_in, (d_send, d_recv))
    down.send_y(1)
    down.send_y(2)
    down.step(1)
    down.send_y(3)
    down.send_y(4)
    grad_out = cot[...].astype(jnp.float32)
    inner, gain_grad, shift_grad = norm_back(first.total(), mid[...], vec[3:4])
    grad = grad_out + inner
    grad_mid[...] = grad
    block_of(attn_full, here.t, rows, 0)[...] = grad.astype(jnp.bfloat16)
    spread = TensorGather(here, attn_full, rows, a_send, a_recv)
    spread.start()
    down.step(2)
    zero = jnp.zeros_like(gain_grad)
    sums[0:1] = zero
    sums[1:2] = zero
    sums[2:3] = jnp.sum(grad, axis=0, keepdims=True)
    sums[3:4] = gain_grad
    sums[4:5] = shift_grad
    sums[5:6] = jnp.sum(grad_out, axis=0, keepdims=True)
    sums[6:7] = zero
    sums[7:8] = zero
    down.step(3)
    spread.finish()
    down.finish()
    first.finish()


def last_kernel(
    part, part_mlp, tok, mid, grad_mid, vec, sums, bias_rows, grad_out, grad_up, grad_qkv,
    grad_tok, result, total_small, total_out, total_up, total_qkv,
    buf, buf_mlp, small_part, small_mine, small_sum, small_buf,
    t_send, t_recv, m_send, m_recv, v_send, v_recv, *scratch
):
    here = Place()
    here.barrier()
    owned = scratch[20:26]
    part_own, mlp_own, mid_own, grad_own, part_sem, mlp_sem, mid_sem, grad_sem = scratch[26:]
    plan = ((grad_out, total_out, 1), (grad_up, total_up, 0), (grad_qkv, total_qkv, 0))
    big = []
    for i, (ref, total, axis) in enumerate(plan):
        group = scratch[5 * i : 5 * i + 5]
        item = DpScatter(
            here, ref, total, axis, *group[:3], group[3:], owned[2 * i : 2 * i + 2]
        )
        item.send_y(1)
        big.append(item)
    scatter = TensorScatter(here, part, buf, t_send, t_recv, (part_own, part_sem))
    scatter.start()
    second = TensorScatter(here, part_mlp, buf_mlp, m_send, m_recv, (mlp_own, mlp_sem))
    second.start()
    mid_copy = pltpu.make_async_copy(mid, mid_own, mid_sem)
    mid_copy.start()
    grad_copy = pltpu.make_async_copy(grad_mid, grad_own, grad_sem)
    grad_copy.start()
    for item in big:
        item.send_y(2)
    for item in big:
        item.step(1)
        item.send_y(3)
    inner, gain_grad, shift_grad = norm_back(
        scatter.total(), tok[...].astype(jnp.float32), vec[0:1]
    )
    grad_copy.wait()
    grad_tok[...] = (grad_own[...] + inner).astype(jnp.bfloat16)
    width = total_small.shape[1]
    for d in range(Z_COUNT * Y_COUNT):
        cols = slice(d * width, (d + 1) * width)
        small_part[8 * d : 8 * d + 8] = sums[:, cols] + bias_rows[8 * d : 8 * d + 8]
        small_part[8 * d : 8 * d + 1] = gain_grad[:, cols]
        small_part[8 * d + 1 : 8 * d + 2] = shift_grad[:, cols]
    group = scratch[15:20]
    small = DpScatter(here, small_part, small_mine, 0, *group[:3], group[3:])
    for k in range(1, Z_COUNT + 1):
        small.send_y(k)
    for item in big:
        item.step(2)
        item.send_y(4)
    small.step(1)
    mid_copy.wait()
    result[...] = (mid_own[...] + second.total() + vec[5:6]).astype(jnp.bfloat16)
    small.step(2)
    for item in big:
        item.step(3)
    small.step(3)
    small.finish()
    small_sum[...] = small_mine[...]
    flights = []
    for k in range(1, T_COUNT):
        flight = remote(
            small_sum, small_buf.at[k - 1], v_send.at[k - 1], v_recv.at[k - 1], here.t_peer(k)
        )
        flight.start()
        flights.append(flight)
    for item in big:
        item.finish()
    for flight in flights:
        flight.wait_recv()
    everyone = small_mine[...] + small_buf[0] + small_buf[1] + small_buf[2]
    row = lax.broadcasted_iota(jnp.int32, everyone.shape, 0)
    total_small[...] = jnp.where(row < 6, everyone, small_mine[...])
    for flight in flights:
        flight.wait_send()
    scatter.finish()
    second.finish()


def on_device_direct(
    tokens, cotangent, seg_lengths, vectors, w_qkv, qv_bias, w_out, w_up, up_bias, w_down
):
    bf16, f32 = jnp.bfloat16, jnp.float32
    rows, width = tokens.shape
    heads, head_part = qv_bias.shape[1], qv_bias.shape[2]
    dp, cols = Z_COUNT * Y_COUNT, vectors.shape[1]
    head_size = head_part * dp
    group_size = rows * T_COUNT
    local_width = w_qkv.shape[2]
    hidden = w_up.shape[1]
    up_part = up_bias.shape[1]
    lengths = seg_lengths[0]
    shape = jax.ShapeDtypeStruct
    qkv_wide = 3 * local_width
    qv_row = jnp.pad(qv_bias.reshape(1, -1), ((0, 0), (0, cols - qv_bias.size)))
    small = jnp.concatenate(
        [vectors, qv_row, up_bias.reshape(1, cols), jnp.zeros((8, cols), f32)]
    ).astype(bf16)
    tok_full, cot_full, small_full, qkv_full, out_full, up_full = call(
        gather_kernel,
        "gather_inputs",
        [
            shape((group_size, width), bf16),
            shape((group_size, width), bf16),
            shape((dp * 16, cols), bf16),
            shape((width, qkv_wide), bf16),
            shape((local_width, width), bf16),
            shape((width, hidden), bf16),
        ],
        [ANYWHERE] * 6,
        [ANYWHERE] * 6,
        gather_sems * 4 + tensor_sems * 2 + [DMA, DMA],
        1,
    )(tokens, cotangent, small, w_qkv.reshape(-1, qkv_wide), w_out, w_up)
    small_full = small_full.reshape(dp, 16, cols).astype(f32)
    vec_full = small_full[:, :8].transpose(1, 0, 2).reshape(8, width)
    bias_full = (
        small_full[:, 6, : qv_bias.size]
        .reshape(dp, 2, heads, head_part)
        .transpose(1, 2, 0, 3)
        .reshape(2, local_width)
    )
    upbias_full = small_full[:, 7].reshape(dp, heads, up_part).transpose(1, 0, 2).reshape(hidden)

    head_ids = lax.axis_index("tensor") * heads + jnp.arange(heads, dtype=jnp.int32)
    slopes = jnp.exp2(-8.0 * (head_ids + 1).astype(f32) / (heads * T_COUNT))
    group_one = layer_norm(tok_full.astype(f32), vec_full[0], vec_full[1]).astype(bf16)
    projected = jnp.dot(group_one, qkv_full, preferred_element_type=f32)
    projected = projected.reshape(group_size, 3, local_width)
    head_shape = (group_size, heads, head_size)
    query_heads = (projected[:, 0] + bias_full[0]).astype(bf16).reshape(head_shape)
    key_heads = projected[:, 1].astype(bf16).reshape(head_shape)
    value_heads = (projected[:, 2] + bias_full[1]).astype(bf16).reshape(head_shape)
    scores = block_scores(query_heads, key_heads, 0, slopes, lengths)
    row_max = jnp.max(scores, axis=-1, keepdims=True)
    exponent = jnp.exp(scores - row_max)
    row_sum = jnp.sum(exponent, axis=-1, keepdims=True)
    probs = exponent / row_sum
    weights = probs.astype(bf16)
    attended = (
        jnp.einsum("hqk,khd->qhd", weights, value_heads, preferred_element_type=f32)
        .reshape(group_size, local_width)
        .astype(bf16)
    )
    part_attn = jnp.dot(attended, out_full, preferred_element_type=f32).astype(bf16)

    middle, group_two, down_full = call(
        middle_kernel,
        "middle",
        [
            shape((rows, width), f32),
            shape((group_size, width), bf16),
            shape((hidden, width), bf16),
        ],
        [IN_VMEM, IN_VMEM, IN_VMEM, ANYWHERE],
        [IN_VMEM, IN_VMEM, ANYWHERE],
        [pltpu.VMEM((3, rows, width), bf16)] + gather_sems + tensor_sems * 2,
        2,
    )(part_attn, tokens, vec_full, w_down)

    contract_rows = (((0,), (0,)), ((), ()))
    contract_cols = (((1,), (1,)), ((), ()))
    pre_act = jnp.dot(group_two, up_full, preferred_element_type=f32) + upbias_full
    activated, gelu_back = jax.vjp(gelu_tanh, pre_act)
    activated = activated.astype(bf16)
    part_mlp = jnp.dot(activated, down_full, preferred_element_type=f32).astype(bf16)
    grad_act = lax.dot_general(cot_full, down_full, contract_cols, preferred_element_type=f32)
    grad_pre = gelu_back(grad_act)[0].astype(bf16)
    part_norm = lax.dot_general(
        grad_pre, up_full, contract_cols, preferred_element_type=f32
    ).astype(bf16)
    grad_down = lax.dot_general(
        activated, cot_full, contract_rows, preferred_element_type=f32
    ).astype(bf16)
    grad_up = lax.dot_general(
        group_two, grad_pre, contract_rows, preferred_element_type=f32
    ).astype(bf16)
    grad_upbias = jnp.sum(grad_pre.astype(f32), axis=0)

    grad_middle, attn_full, sums, total_down = call(
        back_kernel,
        "back",
        [
            shape((rows, width), f32),
            shape((group_size, width), bf16),
            shape((8, width), f32),
            shape((hidden, cols), f32),
        ],
        [IN_VMEM] * 5,
        [IN_VMEM] * 4,
        [pltpu.VMEM((3, rows, width), bf16)]
        + scatter_scratch((hidden, cols), bf16)
        + tensor_sems * 2,
        3,
    )(part_norm, middle, cotangent, vec_full, grad_down)

    grad_out = lax.dot_general(
        attended, attn_full, contract_rows, preferred_element_type=f32
    ).astype(bf16)
    grad_heads = (
        lax.dot_general(attn_full, out_full, contract_cols, preferred_element_type=f32)
        .astype(bf16)
        .reshape(head_shape)
    )
    score_scale = head_size ** (-0.5)
    grad_probs = jnp.einsum("qhd,khd->hqk", grad_heads, value_heads, preferred_element_type=f32)
    row_term = jnp.sum(probs * grad_probs, axis=-1, keepdims=True)
    grad_scores = (probs * (grad_probs - row_term)).astype(bf16)
    grad_query = (
        jnp.einsum("hqk,khd->qhd", grad_scores, key_heads, preferred_element_type=f32) * score_scale
    )
    grad_keys = (
        jnp.einsum("hqk,qhd->khd", grad_scores, query_heads, preferred_element_type=f32)
        * score_scale
    )
    grad_values = jnp.einsum("hqk,qhd->khd", weights, grad_heads, preferred_element_type=f32)
    grad_proj = jnp.concatenate(
        [item.reshape(group_size, local_width).astype(bf16) for item in (grad_query, grad_keys, grad_values)],
        axis=1,
    )
    bias_sums = jnp.sum(grad_proj.astype(f32), axis=0)
    grad_qvbias = jnp.stack([bias_sums[:local_width], bias_sums[2 * local_width :]])
    grad_qkv = lax.dot_general(
        group_one, grad_proj, contract_rows, preferred_element_type=f32
    ).astype(bf16)
    part_first = lax.dot_general(
        grad_proj, qkv_full, contract_cols, preferred_element_type=f32
    ).astype(bf16)
    qv_rows = (
        grad_qvbias.reshape(2, heads, dp, head_part).transpose(2, 0, 1, 3).reshape(dp, 1, qv_bias.size)
    )
    qv_rows = jnp.pad(qv_rows, ((0, 0), (0, 0), (0, cols - qv_bias.size)))
    up_rows = grad_upbias.reshape(heads, dp, up_part).transpose(1, 0, 2).reshape(dp, 1, cols)
    bias_rows = jnp.concatenate([jnp.zeros((dp, 6, cols), f32), qv_rows, up_rows], axis=1)
    bias_rows = bias_rows.reshape(dp * 8, cols)

    grad_tokens, output, total_small, total_out, total_up, total_qkv = call(
        last_kernel,
        "last",
        [
            shape((rows, width), bf16),
            shape((rows, width), bf16),
            shape((8, cols), f32),
            shape((local_width, cols), f32),
            shape((width // dp, hidden), f32),
            shape((3, width // dp, local_width), f32),
        ],
        [ANYWHERE] * 2 + [IN_VMEM] + [ANYWHERE] * 2 + [IN_VMEM] * 3 + [ANYWHERE] * 3,
        [IN_VMEM] * 6,
        [
            pltpu.VMEM((3, rows, width), bf16),
            pltpu.VMEM((3, rows, width), bf16),
            pltpu.VMEM((8 * dp, cols), f32),
            pltpu.VMEM((8, cols), f32),
            pltpu.VMEM((8, cols), f32),
            pltpu.VMEM((3, 8, cols), f32),
        ]
        + tensor_sems * 3
        + scatter_scratch((local_width, cols), bf16)
        + scatter_scratch((width // dp, hidden), bf16)
        + scatter_scratch((width // dp, qkv_wide), bf16)
        + scatter_scratch((8, cols), f32)
        + [pltpu.VMEM((4, local_width, cols), bf16), DMA((4,))]
        + [pltpu.VMEM((4, width // dp, hidden), bf16), DMA((4,))]
        + [pltpu.VMEM((4, width // dp, qkv_wide), bf16), DMA((4,))]
        + [pltpu.VMEM((rows, width), bf16)] * 2
        + [pltpu.VMEM((rows, width), f32)] * 2
        + [DMA] * 4,
        4,
    )(part_first, part_mlp, tokens, middle, grad_middle, vec_full, sums, bias_rows, grad_out, grad_up, grad_qkv)
    return (
        output,
        grad_tokens,
        total_small[:6],
        total_qkv.transpose(1, 0, 2),
        total_small[6, : qv_bias.size].reshape(qv_bias.shape),
        total_out,
        total_up,
        total_small[7].reshape(up_bias.shape),
        total_down,
    )


def solution(mesh):
    direct = mesh.shape["dp"] == Z_COUNT * Y_COUNT and mesh.shape["tensor"] == T_COUNT
    return jax.shard_map(
        on_device_direct if direct else on_device,
        mesh=mesh,
        in_specs=(
            P(("dp", "tensor"), None),
            P(("dp", "tensor"), None),
            P("dp", None),
            P(None, "dp"),
            P("dp", None, "tensor"),
            P(None, "tensor", "dp"),
            P("tensor", "dp"),
            P("dp", "tensor"),
            P("tensor", "dp"),
            P("tensor", "dp"),
        ),
        out_specs=(
            P(("dp", "tensor"), None),
            P(("dp", "tensor"), None),
            P(None, "dp"),
            P("dp", None, "tensor"),
            P(None, "tensor", "dp"),
            P("tensor", "dp"),
            P("dp", "tensor"),
            P("tensor", "dp"),
            P("tensor", "dp"),
        ),
        check_vma=False,
    )
```
